32 devices in a mesh: walk: 16 (over z, y, x), elec: 2 (over core).
Axes of the slice: x: 2, y: 2, z: 4, core: 2. Of those that a mesh axis runs over, the one named last changes fastest.
Arguments:
- hidden: bfloat16 [32, 768, 256], P('walk', 'elec'), may hold values from -12 to 12
- w_query: bfloat16 [256, 256], replicated, may hold values from -0.375 to 0.375
- w_key: bfloat16 [256, 256], replicated, may hold values from -0.375 to 0.375
- w_value: bfloat16 [256, 256], replicated, may hold values from -0.375 to 0.375
- w_out: bfloat16 [256, 256], replicated, may hold values from -0.375 to 0.375
- neighbours: int32 [32, 6, 6], P('walk', 'elec'), may hold values from 0 to 5, as said below
- counts: int32 [32, 6], P('walk', 'elec'), may hold values from 2 to 6, as said below
- cotangent: bfloat16 [32, 768, 256], P('walk', 'elec'), may hold values from -6 to 6
Outputs:
- output: bfloat16 [32, 768, 256], P('walk', 'elec')
- grad_hidden: bfloat16 [32, 768, 256], P('walk', 'elec')
- grad_w_query: float32 [256, 256], replicated
- grad_w_key: float32 [256, 256], replicated
- grad_w_value: float32 [256, 256], replicated
- grad_w_out: float32 [256, 256], replicated
The draws below stay inside these ranges and needn't reach their ends.
Inputs may be any that keep to these rules, and one draw needn't show every extreme that they name: neighbours[w, a, 0] is a itself; the 6 entries of a row are distinct blocks, each held by an index of elec within cyclic distance 1 of the index that holds block a; entries at and past counts[w, a] are ignored. In every draw all counts of the blocks of some index of elec equal 6.
All inputs are finite; a program needn't handle non-finite values.
Results may differ from the reference program's by a relative error of at most 0.012.
The reference program's roundings to bfloat16 on the way count: a program that leaves them out, or rounds other values in their place, can miss the bound.
Values may be sent and summed in bfloat16 or wider, within the bound.
A program may use at most 64 MiB of HBM per device.

```python
import jax
import jax.numpy as jnp
from jax import lax

D = 256
HEADS = 4
HD = 64
BLOCK = 128
MAXN = 6
BLK_DEV = 3
NBLK = 6
ELECTRONS = 768
WALKERS = 32
N_ELEC = 2


def near_offsets(axis_size):
    reach_count = min(2, axis_size // 2)
    offset_list = [0]
    for distance in range(1, reach_count + 1):
        for direction in (1, -1):
            offset = direction * distance % axis_size
            if offset not in offset_list:
                offset_list.append(offset)
    return offset_list


def draw_hidden(key, part):
    first_key = jax.random.fold_in(jax.random.fold_in(key, 3), 0)
    values_drawn = jnp.clip(jax.random.normal(first_key, (WALKERS, ELECTRONS, D), jnp.float32), -6.0, 6.0)
    return values_drawn.astype(jnp.bfloat16)


def draw_neighbours(key, part):
    offset_list = near_offsets(N_ELEC)
    cand_width = len(offset_list) * BLK_DEV
    block_ids = jnp.arange(NBLK, dtype=jnp.int32)
    owner_dev = block_ids // BLK_DEV
    columns = jnp.arange(cand_width, dtype=jnp.int32)
    shifts = jnp.array(offset_list, dtype=jnp.int32)[columns // BLK_DEV]
    candidates = (owner_dev[:, None] - shifts[None, :]) % N_ELEC * BLK_DEV + columns[None, :] % BLK_DEV
    noise = jax.random.randint(jax.random.fold_in(key, 5), (WALKERS, NBLK, cand_width), 0, 1 << 20)
    ranking = noise * cand_width + columns[None, None, :]
    ranking = jnp.where(candidates[None, :, :] == block_ids[None, :, None], -1, ranking)
    order_idx = jnp.argsort(ranking, axis=-1, stable=True)
    picked = jnp.take_along_axis(jnp.broadcast_to(candidates[None, :, :], ranking.shape), order_idx, axis=-1)
    return picked[..., :MAXN].astype(jnp.int32)


def draw_counts(key, part):
    first_key, second_key = jax.random.split(jax.random.fold_in(key, 11))
    drawn = jax.random.randint(first_key, (WALKERS, NBLK), 2, MAXN + 1)
    heavy_dev = jax.random.randint(second_key, (), 0, N_ELEC)
    owner_dev = jnp.arange(NBLK, dtype=jnp.int32) // BLK_DEV
    return jnp.where(owner_dev[None, :] == heavy_dev, MAXN, drawn).astype(jnp.int32)


def shard_levels(key, shape, pieces, least, high):
    level, own = 1.0, jax.random.fold_in(key, 6)
    for dim, parts in pieces:
        draws = jnp.exp(jax.random.uniform(jax.random.fold_in(own, dim), (parts,), jnp.float32, least / len(pieces), high / len(pieces)))
        level = level * jnp.repeat(draws, shape[dim] // parts).reshape([-1 if axis == dim else 1 for axis in range(len(shape))])
    return level


def gaussian(stream_key, extent, spread, limit, cuts=(), held_as=jnp.bfloat16):
    gain = shard_levels(stream_key, extent, cuts, -0.22, 0.18) if cuts else 1.0
    values = jax.random.normal(stream_key, extent, jnp.float32) * spread * gain
    return jnp.minimum(jnp.maximum(values, -limit), limit).astype(held_as)


def setup_inputs(seed: int = 0) -> dict:
    keys = jax.random.split(jax.random.key(seed), 9)
    return {
        "hidden": draw_hidden(jax.random.fold_in(keys[8], 71), 0),
        "w_query": gaussian(keys[1], (D, D), D ** -0.5, 0.375),
        "w_key": gaussian(keys[2], (D, D), D ** -0.5, 0.375),
        "w_value": gaussian(keys[3], (D, D), D ** -0.5, 0.375),
        "w_out": gaussian(keys[4], (D, D), D ** -0.5, 0.375),
        "neighbours": draw_neighbours(jax.random.fold_in(keys[8], 71), 0),
        "counts": draw_counts(jax.random.fold_in(keys[8], 71), 0),
        "cotangent": gaussian(keys[7], (WALKERS, ELECTRONS, D), 1.0, 6.0, ((0, 16), (1, 2))),
    }


NEG_FILL = -1.0e30


def heads_view(array):
    return array.reshape(array.shape[:-1] + (HEADS, HD))


def rounded(array):
    return lax.optimization_barrier(array.astype(jnp.bfloat16)).astype(jnp.float32)


def walker_pass(inputs):
    queries, key_rows, value_rows, nbr_rows, count_row, d_attended = inputs
    scaling = HD ** -0.5
    key_slots = jnp.take(key_rows, nbr_rows, axis=0).reshape(NBLK, MAXN * BLOCK, D)
    value_slots = jnp.take(value_rows, nbr_rows, axis=0).reshape(NBLK, MAXN * BLOCK, D)
    valid_keys = jnp.repeat(jnp.arange(MAXN).astype(jnp.int32)[None, :] < count_row[:, None], BLOCK, axis=1)
    query_wide = heads_view(queries).astype(jnp.float32)
    key_wide = heads_view(key_slots).astype(jnp.float32)
    value_wide = heads_view(value_slots).astype(jnp.float32)
    scores = jnp.einsum("abhd,akhd->ahbk", query_wide, key_wide, precision=lax.Precision.HIGHEST) * scaling
    scores = jnp.where(valid_keys[:, None, None, :], scores, NEG_FILL)
    row_max = jnp.max(scores, axis=-1, keepdims=True)
    log_total = row_max + jnp.log(jnp.sum(jnp.exp(scores - row_max), axis=-1, keepdims=True))
    probabilities = jnp.exp(scores - log_total)
    weight_wide = rounded(probabilities)
    attended = jnp.einsum("ahbk,akhd->abhd", weight_wide, value_wide, precision=lax.Precision.HIGHEST).astype(jnp.bfloat16)
    grad_wide = heads_view(d_attended).astype(jnp.float32)
    d_weights = jnp.einsum("abhd,akhd->ahbk", grad_wide, value_wide, precision=lax.Precision.HIGHEST)
    inner_sum = jnp.transpose(jnp.sum(grad_wide * attended.astype(jnp.float32), axis=-1), (0, 2, 1))
    score_grad = rounded(probabilities * (d_weights - inner_sum[..., None]))
    d_query = (jnp.einsum("ahbk,akhd->abhd", score_grad, key_wide, precision=lax.Precision.HIGHEST) * scaling).astype(jnp.bfloat16)
    key_terms = jnp.einsum("ahbk,abhd->akhd", score_grad, query_wide, precision=lax.Precision.HIGHEST) * scaling
    value_terms = jnp.einsum("ahbk,abhd->akhd", weight_wide, grad_wide, precision=lax.Precision.HIGHEST)
    owner_rows = nbr_rows.reshape(N_ELEC, BLK_DEV * MAXN)
    onehot = (owner_rows[..., None] == jnp.arange(NBLK).astype(jnp.int32)[None, None, :]).astype(jnp.float32)

    def settle(contribution):
        grouped = contribution.reshape(N_ELEC, BLK_DEV * MAXN, BLOCK * D)
        partial_sum = jnp.einsum("esn,esx->enx", onehot, grouped, precision=lax.Precision.HIGHEST)
        return jnp.sum(rounded(partial_sum), axis=0).astype(jnp.bfloat16).reshape(NBLK, BLOCK, D)

    return (attended.reshape(NBLK, BLOCK, D), d_query.reshape(NBLK, BLOCK, D), settle(key_terms), settle(value_terms))


def reference(hidden, w_query, w_key, w_value, w_out, neighbours, counts, cotangent):
    all_rows = hidden.reshape(WALKERS * ELECTRONS, D)

    def project(weight):
        product = jnp.dot(all_rows, weight, preferred_element_type=jnp.float32)
        return product.astype(jnp.bfloat16).reshape(WALKERS, NBLK, BLOCK, D)

    queries = project(w_query)
    key_rows = project(w_key)
    value_rows = project(w_value)
    cot_rows = cotangent.reshape(WALKERS * ELECTRONS, D)
    d_attended = jnp.dot(cot_rows, w_out.T, preferred_element_type=jnp.float32).astype(jnp.bfloat16)
    d_attended = d_attended.reshape(WALKERS, NBLK, BLOCK, D)
    attended, d_query, d_key, d_value = lax.map(walker_pass, (queries, key_rows, value_rows, neighbours, counts, d_attended))
    attended_rows = attended.reshape(-1, D)
    query_grad_rows = d_query.reshape(-1, D)
    key_grad_rows = d_key.reshape(-1, D)
    value_grad_rows = d_value.reshape(-1, D)
    output = (all_rows.astype(jnp.float32) + jnp.dot(attended_rows, w_out, preferred_element_type=jnp.float32)).astype(jnp.bfloat16)
    grad_hidden = cot_rows.astype(jnp.float32) + jnp.dot(query_grad_rows, w_query.T, preferred_element_type=jnp.float32)
    grad_hidden = grad_hidden + jnp.dot(key_grad_rows, w_key.T, preferred_element_type=jnp.float32)
    grad_hidden = grad_hidden + jnp.dot(value_grad_rows, w_value.T, preferred_element_type=jnp.float32)
    grad_hidden = grad_hidden.astype(jnp.bfloat16)
    grad_w_query = jnp.dot(all_rows.T, query_grad_rows, preferred_element_type=jnp.float32) / WALKERS
    grad_w_key = jnp.dot(all_rows.T, key_grad_rows, preferred_element_type=jnp.float32) / WALKERS
    grad_w_value = jnp.dot(all_rows.T, value_grad_rows, preferred_element_type=jnp.float32) / WALKERS
    grad_w_out = jnp.dot(attended_rows.T, cot_rows, preferred_element_type=jnp.float32) / WALKERS
    shape_full = (WALKERS, ELECTRONS, D)
    return (output.reshape(shape_full), grad_hidden.reshape(shape_full), grad_w_query, grad_w_key, grad_w_value, grad_w_out)
```

```python
import jax
import jax.numpy as jnp
from jax import lax
from jax.experimental import pallas as pl
from jax.experimental.pallas import tpu as pltpu
from jax.sharding import PartitionSpec as P

HD = 64
BLOCK = 128


NEG_FILL = -1e30


def split_heads(array, head_count):
    return array.reshape(array.shape[:-1] + (head_count, array.shape[-1] // head_count))


def masked_scores(query_blk, key_slots, valid_keys, head_count, scaling):
    scores = (
        jnp.einsum(
            "bhd,khd->hbk",
            split_heads(query_blk, head_count),
            split_heads(key_slots, head_count),
            preferred_element_type=jnp.float32,
        )
        * scaling
    )
    return jnp.where(valid_keys[None, None, :], scores, NEG_FILL)


def body(hidden, w_query, w_key, w_value, w_out, neighbours, counts, cotangent):
    walk_dev, local_rows, model_width = hidden.shape
    blocks = neighbours.shape[1]
    slot_count = neighbours.shape[2]
    head_count = model_width // HD
    scaling = HD ** (-0.5)
    all_rows = hidden.reshape(-1, model_width)
    joined = jnp.concatenate([w_query, w_key, w_value], axis=1)
    projected = jnp.dot(all_rows, joined, preferred_element_type=jnp.float32).astype(jnp.bfloat16)
    query_rows = projected[:, :model_width]
    key_blocks = projected[:, model_width : 2 * model_width].reshape(
        walk_dev, blocks, BLOCK, model_width
    )
    value_blocks = projected[:, 2 * model_width :].reshape(walk_dev, blocks, BLOCK, model_width)
    cot_rows = cotangent.reshape(-1, model_width)
    d_attended = jnp.dot(cot_rows, w_out.T, preferred_element_type=jnp.float32).astype(jnp.bfloat16)
    key_store, value_store = (
        lax.all_gather(key_blocks, "elec", axis=1, tiled=True),
        lax.all_gather(value_blocks, "elec", axis=1, tiled=True),
    )
    stored = key_store.shape[1]
    walker_base = stored * jnp.arange(walk_dev, dtype=jnp.int32)[:, None, None]
    flat_slots = (neighbours + walker_base).reshape(-1, slot_count)
    key_flat = key_store.reshape(-1, BLOCK, model_width)
    value_flat = value_store.reshape(-1, BLOCK, model_width)
    query_items = query_rows.reshape(-1, BLOCK, model_width)
    count_items = counts.reshape(-1)
    grad_items = d_attended.reshape(-1, BLOCK, model_width)

    def slot_rows(flat_row, live_count):
        key_slots = jnp.take(key_flat, flat_row, axis=0).reshape(slot_count * BLOCK, model_width)
        value_slots = jnp.take(value_flat, flat_row, axis=0).reshape(
            slot_count * BLOCK, model_width
        )
        valid_keys = jnp.repeat(jnp.arange(slot_count, dtype=jnp.int32) < live_count, BLOCK)
        return (key_slots, value_slots, valid_keys)

    def forward_item(inputs):
        query_blk, flat_row, live_count = inputs
        key_slots, value_slots, valid_keys = slot_rows(flat_row, live_count)
        scores = masked_scores(query_blk, key_slots, valid_keys, head_count, scaling)
        row_max = jnp.max(scores, axis=-1, keepdims=True)
        log_total = row_max + jnp.log(jnp.sum(jnp.exp(scores - row_max), axis=-1, keepdims=True))
        weights = jnp.exp(scores - log_total).astype(jnp.bfloat16)
        attended = jnp.einsum(
            "hbk,khd->bhd",
            weights,
            split_heads(value_slots, head_count),
            preferred_element_type=jnp.float32,
        )
        return (attended.astype(jnp.bfloat16).reshape(BLOCK, model_width), log_total)

    attended_items, log_items = lax.map(forward_item, (query_items, flat_slots, count_items))
    attended_rows = attended_items.reshape(-1, model_width)
    output = (
        all_rows.astype(jnp.float32)
        + jnp.dot(attended_rows, w_out, preferred_element_type=jnp.float32)
    ).astype(jnp.bfloat16)
    walkers_all = walk_dev * lax.axis_size("walk")
    grad_out = jnp.dot(attended_rows.T, cot_rows, preferred_element_type=jnp.float32) / walkers_all

    def backward_item(inputs):
        query_blk, flat_row, live_count, attended_blk, log_total, grad_blk = inputs
        key_slots, value_slots, valid_keys = slot_rows(flat_row, live_count)
        scores = masked_scores(query_blk, key_slots, valid_keys, head_count, scaling)
        probabilities = jnp.exp(scores - log_total)
        weights = probabilities.astype(jnp.bfloat16)
        grad_heads = split_heads(grad_blk, head_count)
        d_weights = jnp.einsum(
            "bhd,khd->hbk",
            grad_heads,
            split_heads(value_slots, head_count),
            preferred_element_type=jnp.float32,
        )
        inner_sum = jnp.sum(
            grad_heads.astype(jnp.float32)
            * split_heads(attended_blk, head_count).astype(jnp.float32),
            axis=-1,
        ).T
        score_grad = (probabilities * (d_weights - inner_sum[..., None])).astype(jnp.bfloat16)
        d_query = (
            jnp.einsum(
                "hbk,khd->bhd",
                score_grad,
                split_heads(key_slots, head_count),
                preferred_element_type=jnp.float32,
            )
            * scaling
        )
        key_terms = (
            jnp.einsum(
                "hbk,bhd->khd",
                score_grad,
                split_heads(query_blk, head_count),
                preferred_element_type=jnp.float32,
            )
            * scaling
        )
        value_terms = jnp.einsum(
            "hbk,bhd->khd", weights, grad_heads, preferred_element_type=jnp.float32
        )
        return (
            d_query.astype(jnp.bfloat16).reshape(BLOCK, model_width),
            key_terms.reshape(-1, model_width),
            value_terms.reshape(-1, model_width),
        )

    query_grad_items, key_terms, value_terms = lax.map(
        backward_item, (query_items, flat_slots, count_items, attended_items, log_items, grad_items)
    )
    onehot = (
        neighbours.reshape(walk_dev, blocks * slot_count)[..., None]
        == jnp.arange(stored, dtype=jnp.int32)[None, None, :]
    ).astype(jnp.float32)

    def place(contribution):
        grouped = contribution.reshape(walk_dev, blocks * slot_count, BLOCK * model_width)
        placed = jnp.einsum("wsn,wsx->wnx", onehot, grouped, precision=lax.Precision.HIGHEST)
        return placed.reshape(walk_dev, stored, BLOCK, model_width).astype(jnp.bfloat16)

    key_round = place(key_terms)
    value_round = place(value_terms)
    key_wide = lax.optimization_barrier(key_round).astype(jnp.float32)
    value_wide = lax.optimization_barrier(value_round).astype(jnp.float32)
    key_sum, value_sum = (
        lax.psum_scatter(
            key_wide.astype(jnp.bfloat16), "elec", scatter_dimension=1, tiled=True
        ).astype(jnp.float32),
        lax.psum_scatter(
            value_wide.astype(jnp.bfloat16), "elec", scatter_dimension=1, tiled=True
        ).astype(jnp.float32),
    )
    key_grad_rows = key_sum.astype(jnp.bfloat16).reshape(-1, model_width)
    value_grad_rows = value_sum.astype(jnp.bfloat16).reshape(-1, model_width)
    query_grad_rows = query_grad_items.reshape(-1, model_width)
    grad_hidden = cot_rows.astype(jnp.float32) + jnp.dot(
        query_grad_rows, w_query.T, preferred_element_type=jnp.float32
    )
    grad_hidden = grad_hidden + jnp.dot(key_grad_rows, w_key.T, preferred_element_type=jnp.float32)
    grad_hidden = grad_hidden + jnp.dot(
        value_grad_rows, w_value.T, preferred_element_type=jnp.float32
    )
    grad_hidden = grad_hidden.astype(jnp.bfloat16).reshape(hidden.shape)
    grad_query = (
        jnp.dot(all_rows.T, query_grad_rows, preferred_element_type=jnp.float32) / walkers_all
    )
    grad_key = jnp.dot(all_rows.T, key_grad_rows, preferred_element_type=jnp.float32) / walkers_all
    grad_value = (
        jnp.dot(all_rows.T, value_grad_rows, preferred_element_type=jnp.float32) / walkers_all
    )
    grad_query, grad_key, grad_value, grad_out = lax.psum(
        (grad_query, grad_key, grad_value, grad_out), ("walk", "elec")
    )
    return (output.reshape(hidden.shape), grad_hidden, grad_query, grad_key, grad_value, grad_out)


F32 = jnp.float32
BF16 = jnp.bfloat16
PAIR = 2 * HD


def dot_nn(a, b):
    return lax.dot_general(a, b, (((1,), (0,)), ((), ())), preferred_element_type=F32)


def dot_nt(a, b):
    return lax.dot_general(a, b, (((1,), (1,)), ((), ())), preferred_element_type=F32)


def by_head(block):
    lane = lax.broadcasted_iota(jnp.int32, block.shape, 1)
    zero = jnp.zeros_like(block)
    return jnp.concatenate(
        [jnp.where(lane < HD, block, zero), jnp.where(lane < HD, zero, block)], axis=0
    )


def walker_kernel(
    nbr, cnt, hid, cot, wq, wk, wv, wo, out, grad, gw,
    hs, cs, bs, bsend, q_s, k_s, v_s, da_s, kt_s, vt_s, dat_s,
    at_s, att_s, dqt_s, dq_s, w_s, ds_s, qb_s, db_s, kp_s, vp_s, dk_s, dv_s, ht_s, osend, gsend,
    send_sem, recv_sem, local_sem, osem_s, osem_r,
):
    e = lax.axis_index("elec")
    other = 1 - e
    blocks = hid.shape[1] // BLOCK
    slots = nbr.shape[2]
    n_blocks = 2 * blocks
    half = hid.shape[1]
    rows = 2 * half
    pairs = hid.shape[2] // PAIR

    barrier = pltpu.get_barrier_semaphore()
    pl.semaphore_signal(barrier, inc=1, device_id={"elec": other}, device_id_type=pl.DeviceIdType.MESH)

    lane = lax.broadcasted_iota(jnp.int32, (16, 128), 1)
    sub = lax.broadcasted_iota(jnp.int32, (16, 128), 0)
    for w in range(2):
        bias = jnp.full((16, 128), NEG_FILL, F32)
        for a in range(blocks):
            for j in range(slots):
                live = jnp.where(j < cnt[w, a], nbr[w, a, j], -1)
                bias = jnp.where((sub == a) & (lane == live), 0.0, bias)
        bsend[w] = bias.astype(BF16)

    pl.semaphore_wait(barrier, 1)
    sends = []
    for i, (src, dst) in enumerate(((hid, hs), (cot, cs), (bsend, bs))):
        copy = pltpu.make_async_remote_copy(
            src_ref=src.at[other], dst_ref=dst.at[e], send_sem=send_sem.at[i], recv_sem=recv_sem.at[i],
            device_id={"elec": other}, device_id_type=pl.DeviceIdType.MESH,
        )
        copy.start()
        sends.append(copy)

    hs[e] = hid[e]
    cs[e] = cot[e]
    bs[e] = bsend[e]

    def project(h):
        rows_h = hs[h]
        q_s[h] = (dot_nn(rows_h, wq[...]).astype(BF16).astype(F32) * HD ** (-0.5)).astype(BF16)
        k_s[h] = dot_nn(rows_h, wk[...]).astype(BF16)
        v_s[h] = dot_nn(rows_h, wv[...]).astype(BF16)
        da_s[h] = dot_nt(cs[h], wo[...]).astype(BF16)

    project(e)
    for copy in sends:
        copy.wait()
    project(other)

    k_all = k_s[...].reshape(rows, -1)
    v_all = v_s[...].reshape(rows, -1)
    kt = k_all.T
    vt = v_all.T
    dat = da_s[...].reshape(rows, -1).T
    which = (
        lax.broadcasted_iota(jnp.int32, (rows, 128), 0) // BLOCK
        == lax.broadcasted_iota(jnp.int32, (rows, 128), 1)
    )
    onehot = jnp.where(which, 1.0, 0.0).astype(BF16)
    for p in range(pairs):
        lanes = slice(p * PAIR, (p + 1) * PAIR)
        kp_s[p, :, :PAIR] = k_all[:, lanes]
        kp_s[p, :, PAIR:] = onehot
        vp_s[p] = v_all[:, lanes]
        kt_s[p] = kt[lanes]
        vt_s[p] = vt[lanes]
        for a in range(n_blocks):
            dat_s[p, a] = dat[lanes, a * BLOCK : (a + 1) * BLOCK]
            r = slice((a % blocks) * BLOCK, (a % blocks + 1) * BLOCK)
            qb_s[p, a // blocks, a % blocks] = by_head(q_s[a // blocks, r, lanes])
            db_s[p, a // blocks, a % blocks] = by_head(da_s[a // blocks, r, lanes])

    def group(step, carry):
        p = step // 2
        g = step % 2
        for i in range(blocks):
            a = g * blocks + i
            q2 = qb_s[p, g, i]
            d2 = db_s[p, g, i]
            bias = jnp.broadcast_to(bs[g, i : i + 1, :], (2 * BLOCK, 128))
            scores = dot_nt(kp_s[p], jnp.concatenate([q2, bias], axis=1))
            top = jnp.max(scores, axis=0, keepdims=True)
            expo = jnp.exp(scores - top)
            prob = expo * (1.0 / jnp.sum(expo, axis=0, keepdims=True))
            weights = prob.astype(BF16)
            cols = slice(i * 2 * BLOCK, (i + 1) * 2 * BLOCK)
            w_s[:, cols] = weights
            mixed = dot_nn(vt_s[p], weights)
            att = jnp.concatenate([mixed[:HD, :BLOCK], mixed[HD:, BLOCK:]], axis=0).astype(BF16)
            prod = att.astype(F32) * dat_s[p, a].astype(F32)
            inner = jnp.concatenate(
                [
                    jnp.sum(prod[:HD], axis=0, keepdims=True),
                    jnp.sum(prod[HD:], axis=0, keepdims=True),
                ],
                axis=1,
            )
            at_s[p, a] = att
            att_s[p, g, i] = att.T
            d_scores = (prob * (dot_nt(vp_s[p], d2) - inner)).astype(BF16)
            ds_s[:, cols] = d_scores
            mixed = dot_nn(kt_s[p], d_scores)
            dqt = jnp.concatenate([mixed[:HD, :BLOCK], mixed[HD:, BLOCK:]], axis=0)
            dqt = (dqt * HD ** (-0.5)).astype(BF16)
            dqt_s[p, a] = dqt
            dq_s[p, g, i] = dqt.T
        dk_s[g, p] = dot_nn(ds_s[...], qb_s[p, g].reshape(-1, PAIR)).astype(BF16)
        dv_s[g, p] = dot_nn(w_s[...], db_s[p, g].reshape(-1, PAIR)).astype(BF16)
        return carry

    lax.fori_loop(0, 2 * pairs, group, 0)

    def whole(ref):
        return jnp.concatenate([ref[p].reshape(rows, PAIR) for p in range(pairs)], axis=1)

    h_all = hs[...].reshape(rows, -1)
    c_all = cs[...].reshape(rows, -1)
    ht = h_all.T
    ht_s[...] = ht

    def summed(ref):
        return jnp.concatenate(
            [(ref[0, p].astype(F32) + ref[1, p].astype(F32)).astype(BF16) for p in range(pairs)],
            axis=1,
        )

    attended = whole(att_s)
    d_query = whole(dq_s)
    d_key = summed(dk_s)
    d_value = summed(dv_s)
    result = (h_all.astype(F32) + dot_nn(attended, wo[...])).astype(BF16)
    osend[...] = result.reshape(osend.shape)
    back = (
        c_all.astype(F32)
        + dot_nt(d_query, wq[...])
        + dot_nt(d_key, wk[...])
        + dot_nt(d_value, wv[...])
    ).astype(BF16)
    gsend[...] = back.reshape(gsend.shape)
    sends = []
    for i, (src, dst) in enumerate(((osend, out), (gsend, grad))):
        copy = pltpu.make_async_remote_copy(
            src_ref=src.at[other], dst_ref=dst.at[e], send_sem=osem_s.at[i], recv_sem=osem_r.at[i],
            device_id={"elec": other}, device_id_type=pl.DeviceIdType.MESH,
        )
        copy.start()
        sends.append(copy)
    out[e] = osend[e]
    grad[e] = gsend[e]
    gw[0] = dot_nn(ht_s[...], d_query)
    gw[1] = dot_nn(ht_s[...], d_key)
    gw[2] = dot_nn(ht_s[...], d_value)
    at = jnp.concatenate(
        [
            jnp.concatenate([at_s[p, a] for a in range(n_blocks)], axis=1)
            for p in range(pairs)
        ],
        axis=0,
    )
    gw[3] = dot_nn(at, c_all)
    for copy in sends:
        copy.wait()


def pair_body(hidden, w_query, w_key, w_value, w_out, neighbours, counts, cotangent):
    half, width = hidden.shape[1:]
    blocks = half // BLOCK
    rows, pairs, n_blocks = 2 * half, width // PAIR, 2 * blocks
    vmem = pl.BlockSpec(memory_space=pltpu.VMEM)
    smem = pl.BlockSpec(memory_space=pltpu.SMEM)
    both = (2, half, width)
    by_pair = (pairs, 2, blocks, BLOCK, PAIR)
    by_pair2 = (pairs, 2, blocks, 2 * BLOCK, PAIR)

    def buf(*shape, dtype=BF16):
        return pltpu.VMEM(shape, dtype)

    out, grad, gw = pl.pallas_call(
        walker_kernel,
        out_shape=(
            jax.ShapeDtypeStruct(hidden.shape, BF16),
            jax.ShapeDtypeStruct(hidden.shape, BF16),
            jax.ShapeDtypeStruct((4, width, width), F32),
        ),
        in_specs=[smem, smem] + [vmem] * 6,
        out_specs=(vmem, vmem, vmem),
        scratch_shapes=[
            buf(*both), buf(*both), buf(2, 16, 128), buf(2, 16, 128),
            buf(*both), buf(*both), buf(*both), buf(*both),
            buf(pairs, PAIR, rows), buf(pairs, PAIR, rows), buf(pairs, n_blocks, PAIR, BLOCK),
            buf(pairs, n_blocks, PAIR, BLOCK), buf(*by_pair),
            buf(pairs, n_blocks, PAIR, BLOCK), buf(*by_pair),
            buf(rows, blocks * 2 * BLOCK), buf(rows, blocks * 2 * BLOCK),
            buf(*by_pair2), buf(*by_pair2),
            buf(pairs, rows, 2 * PAIR), buf(pairs, rows, PAIR),
            buf(2, pairs, rows, PAIR), buf(2, pairs, rows, PAIR),
            buf(width, rows), buf(*both), buf(*both),
            pltpu.SemaphoreType.DMA((3,)), pltpu.SemaphoreType.DMA((3,)),
            pltpu.SemaphoreType.DMA((2,)),
            pltpu.SemaphoreType.DMA((2,)), pltpu.SemaphoreType.DMA((2,)),
        ],
        compiler_params=pltpu.CompilerParams(
            collective_id=0, has_side_effects=True, vmem_limit_bytes=48 * 1024 * 1024
        ),
    )(neighbours, counts, hidden, cotangent, w_query, w_key, w_value, w_out)
    walkers_all = hidden.shape[0] * lax.axis_size("walk")
    gw = lax.psum(gw, ("walk", "elec")) / walkers_all
    return out, grad, gw[0], gw[1], gw[2], gw[3]


def any_body(hidden, *rest):
    blocks = rest[4].shape[1]
    if lax.axis_size("elec") == 2 and hidden.shape[0] == 2 and 2 * blocks <= 128 and blocks <= 16:
        return pair_body(hidden, *rest)
    return body(hidden, *rest)


def solution(mesh):
    placed = (
        P("walk", "elec", None),
        P(),
        P(),
        P(),
        P(),
        P("walk", "elec", None),
        P("walk", "elec"),
        P("walk", "elec", None),
    )
    return jax.shard_map(
        any_body,
        mesh=mesh,
        in_specs=placed,
        out_specs=(P("walk", "elec", None), P("walk", "elec", None), P(), P(), P(), P()),
        check_vma=False,
    )
```

```python
import jax
import jax.numpy as jnp
from jax import lax
from jax.experimental import pallas as pl
from jax.experimental.pallas import tpu as pltpu
from jax.sharding import PartitionSpec as P

HD = 64
BLOCK = 128


NEG_FILL = -1e30


def split_heads(array, head_count):
    return array.reshape(array.shape[:-1] + (head_count, array.shape[-1] // head_count))


def masked_scores(query_blk, key_slots, valid_keys, head_count, scaling):
    scores = (
        jnp.einsum(
            "bhd,khd->hbk",
            split_heads(query_blk, head_count),
            split_heads(key_slots, head_count),
            preferred_element_type=jnp.float32,
        )
        * scaling
    )
    return jnp.where(valid_keys[None, None, :], scores, NEG_FILL)


def body(hidden, w_query, w_key, w_value, w_out, neighbours, counts, cotangent):
    walk_dev, local_rows, model_width = hidden.shape
    blocks = neighbours.shape[1]
    slot_count = neighbours.shape[2]
    head_count = model_width // HD
    scaling = HD ** (-0.5)
    all_rows = hidden.reshape(-1, model_width)
    joined = jnp.concatenate([w_query, w_key, w_value], axis=1)
    projected = jnp.dot(all_rows, joined, preferred_element_type=jnp.float32).astype(jnp.bfloat16)
    query_rows = projected[:, :model_width]
    key_blocks = projected[:, model_width : 2 * model_width].reshape(
        walk_dev, blocks, BLOCK, model_width
    )
    value_blocks = projected[:, 2 * model_width :].reshape(walk_dev, blocks, BLOCK, model_width)
    cot_rows = cotangent.reshape(-1, model_width)
    d_attended = jnp.dot(cot_rows, w_out.T, preferred_element_type=jnp.float32).astype(jnp.bfloat16)
    key_store, value_store = (
        lax.all_gather(key_blocks, "elec", axis=1, tiled=True),
        lax.all_gather(value_blocks, "elec", axis=1, tiled=True),
    )
    stored = key_store.shape[1]
    walker_base = stored * jnp.arange(walk_dev, dtype=jnp.int32)[:, None, None]
    flat_slots = (neighbours + walker_base).reshape(-1, slot_count)
    key_flat = key_store.reshape(-1, BLOCK, model_width)
    value_flat = value_store.reshape(-1, BLOCK, model_width)
    query_items = query_rows.reshape(-1, BLOCK, model_width)
    count_items = counts.reshape(-1)
    grad_items = d_attended.reshape(-1, BLOCK, model_width)

    def slot_rows(flat_row, live_count):
        key_slots = jnp.take(key_flat, flat_row, axis=0).reshape(slot_count * BLOCK, model_width)
        value_slots = jnp.take(value_flat, flat_row, axis=0).reshape(
            slot_count * BLOCK, model_width
        )
        valid_keys = jnp.repeat(jnp.arange(slot_count, dtype=jnp.int32) < live_count, BLOCK)
        return (key_slots, value_slots, valid_keys)

    def forward_item(inputs):
        query_blk, flat_row, live_count = inputs
        key_slots, value_slots, valid_keys = slot_rows(flat_row, live_count)
        scores = masked_scores(query_blk, key_slots, valid_keys, head_count, scaling)
        row_max = jnp.max(scores, axis=-1, keepdims=True)
        log_total = row_max + jnp.log(jnp.sum(jnp.exp(scores - row_max), axis=-1, keepdims=True))
        weights = jnp.exp(scores - log_total).astype(jnp.bfloat16)
        attended = jnp.einsum(
            "hbk,khd->bhd",
            weights,
            split_heads(value_slots, head_count),
            preferred_element_type=jnp.float32,
        )
        return (attended.astype(jnp.bfloat16).reshape(BLOCK, model_width), log_total)

    attended_items, log_items = lax.map(forward_item, (query_items, flat_slots, count_items))
    attended_rows = attended_items.reshape(-1, model_width)
    output = (
        all_rows.astype(jnp.float32)
        + jnp.dot(attended_rows, w_out, preferred_element_type=jnp.float32)
    ).astype(jnp.bfloat16)
    walkers_all = walk_dev * lax.axis_size("walk")
    grad_out = jnp.dot(attended_rows.T, cot_rows, preferred_element_type=jnp.float32) / walkers_all

    def backward_item(inputs):
        query_blk, flat_row, live_count, attended_blk, log_total, grad_blk = inputs
        key_slots, value_slots, valid_keys = slot_rows(flat_row, live_count)
        scores = masked_scores(query_blk, key_slots, valid_keys, head_count, scaling)
        probabilities = jnp.exp(scores - log_total)
        weights = probabilities.astype(jnp.bfloat16)
        grad_heads = split_heads(grad_blk, head_count)
        d_weights = jnp.einsum(
            "bhd,khd->hbk",
            grad_heads,
            split_heads(value_slots, head_count),
            preferred_element_type=jnp.float32,
        )
        inner_sum = jnp.sum(
            grad_heads.astype(jnp.float32)
            * split_heads(attended_blk, head_count).astype(jnp.float32),
            axis=-1,
        ).T
        score_grad = (probabilities * (d_weights - inner_sum[..., None])).astype(jnp.bfloat16)
        d_query = (
            jnp.einsum(
                "hbk,khd->bhd",
                score_grad,
                split_heads(key_slots, head_count),
                preferred_element_type=jnp.float32,
            )
            * scaling
        )
        key_terms = (
            jnp.einsum(
                "hbk,bhd->khd",
                score_grad,
                split_heads(query_blk, head_count),
                preferred_element_type=jnp.float32,
            )
            * scaling
        )
        value_terms = jnp.einsum(
            "hbk,bhd->khd", weights, grad_heads, preferred_element_type=jnp.float32
        )
        return (
            d_query.astype(jnp.bfloat16).reshape(BLOCK, model_width),
            key_terms.reshape(-1, model_width),
            value_terms.reshape(-1, model_width),
        )

    query_grad_items, key_terms, value_terms = lax.map(
        backward_item, (query_items, flat_slots, count_items, attended_items, log_items, grad_items)
    )
    onehot = (
        neighbours.reshape(walk_dev, blocks * slot_count)[..., None]
        == jnp.arange(stored, dtype=jnp.int32)[None, None, :]
    ).astype(jnp.float32)

    def place(contribution):
        grouped = contribution.reshape(walk_dev, blocks * slot_count, BLOCK * model_width)
        placed = jnp.einsum("wsn,wsx->wnx", onehot, grouped, precision=lax.Precision.HIGHEST)
        return placed.reshape(walk_dev, stored, BLOCK, model_width).astype(jnp.bfloat16)

    key_round = place(key_terms)
    value_round = place(value_terms)
    key_wide = lax.optimization_barrier(key_round).astype(jnp.float32)
    value_wide = lax.optimization_barrier(value_round).astype(jnp.float32)
    key_sum, value_sum = (
        lax.psum_scatter(
            key_wide.astype(jnp.bfloat16), "elec", scatter_dimension=1, tiled=True
        ).astype(jnp.float32),
        lax.psum_scatter(
            value_wide.astype(jnp.bfloat16), "elec", scatter_dimension=1, tiled=True
        ).astype(jnp.float32),
    )
    key_grad_rows = key_sum.astype(jnp.bfloat16).reshape(-1, model_width)
    value_grad_rows = value_sum.astype(jnp.bfloat16).reshape(-1, model_width)
    query_grad_rows = query_grad_items.reshape(-1, model_width)
    grad_hidden = cot_rows.astype(jnp.float32) + jnp.dot(
        query_grad_rows, w_query.T, preferred_element_type=jnp.float32
    )
    grad_hidden = grad_hidden + jnp.dot(key_grad_rows, w_key.T, preferred_element_type=jnp.float32)
    grad_hidden = grad_hidden + jnp.dot(
        value_grad_rows, w_value.T, preferred_element_type=jnp.float32
    )
    grad_hidden = grad_hidden.astype(jnp.bfloat16).reshape(hidden.shape)
    grad_query = (
        jnp.dot(all_rows.T, query_grad_rows, preferred_element_type=jnp.float32) / walkers_all
    )
    grad_key = jnp.dot(all_rows.T, key_grad_rows, preferred_element_type=jnp.float32) / walkers_all
    grad_value = (
        jnp.dot(all_rows.T, value_grad_rows, preferred_element_type=jnp.float32) / walkers_all
    )
    grad_query, grad_key, grad_value, grad_out = lax.psum(
        (grad_query, grad_key, grad_value, grad_out), ("walk", "elec")
    )
    return (output.reshape(hidden.shape), grad_hidden, grad_query, grad_key, grad_value, grad_out)


F32 = jnp.float32
BF16 = jnp.bfloat16
PAIR = 2 * HD


def dot_nn(a, b):
    return lax.dot_general(a, b, (((1,), (0,)), ((), ())), preferred_element_type=F32)


def dot_nt(a, b):
    return lax.dot_general(a, b, (((1,), (1,)), ((), ())), preferred_element_type=F32)


def by_head(block):
    lane = lax.broadcasted_iota(jnp.int32, block.shape, 1)
    zero = jnp.zeros_like(block)
    return jnp.concatenate(
        [jnp.where(lane < HD, block, zero), jnp.where(lane < HD, zero, block)], axis=0
    )


def walker_kernel(
    nbr, cnt, hid, cot, wq_h, wk_h, wv_h, wo_h, out, grad, full,
    wq, wk, wv, wo, hs, cs, bs, bsend, q_s, k_s, v_s, da_s, kt_s, vt_s, dat_s,
    at_s, att_s, dqt_s, dq_s, w_s, ds_s, qb_s, db_s, kp_s, vp_s, dk_s, dv_s, ht_s, osend, gsend,
    g_s, a_s, r0, s1, b1, r1, s2, b2, r2, agz, agxy,
    send_sem, recv_sem, local_sem, osem_s, osem_r, ar_send, ar_recv,
):
    e = lax.axis_index("elec")
    other = 1 - e
    blocks = hid.shape[1] // BLOCK
    slots = nbr.shape[2]
    n_blocks = 2 * blocks
    half = hid.shape[1]
    rows = 2 * half
    pairs = hid.shape[2] // PAIR

    walk = lax.axis_index("walk")
    planes = lax.axis_size("walk") // 4
    plane, spot = walk // 4, walk % 4
    sx, sy = spot % 2, spot // 2
    near = [((sy + r // 2) % 2) * 2 + (sx + r % 2) % 2 for r in range(1, 4)]
    layers = [(plane + r) % planes for r in range(1, planes)]
    spot_ids = [{"walk": plane * 4 + t, "elec": e} for t in near]
    layer_ids = [{"walk": t * 4 + spot, "elec": e} for t in layers]
    core_id = {"walk": walk, "elec": other}
    mesh_ids = pl.DeviceIdType.MESH

    barrier = pltpu.get_barrier_semaphore()
    for peer in [core_id] + spot_ids + layer_ids:
        pl.semaphore_signal(barrier, inc=1, device_id=peer, device_id_type=mesh_ids)

    local = [
        pltpu.make_async_copy(src, dst, local_sem.at[i])
        for i, (src, dst) in enumerate(
            (
                (hid.at[e], hs.at[e]), (wq_h, wq), (wk_h, wk), (wv_h, wv),
                (cot.at[e], cs.at[e]), (wo_h, wo),
            )
        )
    ]
    for copy in local:
        copy.start()

    lane = lax.broadcasted_iota(jnp.int32, (16, 128), 1)
    sub = lax.broadcasted_iota(jnp.int32, (16, 128), 0)
    for w in range(2):
        bias = jnp.full((16, 128), NEG_FILL, F32)
        for a in range(blocks):
            for j in range(slots):
                live = jnp.where(j < cnt[w, a], nbr[w, a, j], -1)
                bias = jnp.where((sub == a) & (lane == live), 0.0, bias)
        bsend[w] = bias.astype(BF16)

    pl.semaphore_wait(barrier, 3 + planes)
    sends = []
    for i, (src, dst) in enumerate(((hid, hs), (cot, cs), (bsend, bs))):
        copy = pltpu.make_async_remote_copy(
            src_ref=src.at[other], dst_ref=dst.at[e], send_sem=send_sem.at[i], recv_sem=recv_sem.at[i],
            device_id={"elec": other}, device_id_type=pl.DeviceIdType.MESH,
        )
        copy.start()
        sends.append(copy)

    bs[e] = bsend[e]
    for copy in local:
        copy.wait()

    def project(h):
        rows_h = hs[h]
        q_s[h] = (dot_nn(rows_h, wq[...]).astype(BF16).astype(F32) * HD ** (-0.5)).astype(BF16)
        k_s[h] = dot_nn(rows_h, wk[...]).astype(BF16)
        v_s[h] = dot_nn(rows_h, wv[...]).astype(BF16)
        da_s[h] = dot_nt(cs[h], wo[...]).astype(BF16)

    project(e)
    for copy in sends:
        copy.wait()
    project(other)

    k_all = k_s[...].reshape(rows, -1)
    v_all = v_s[...].reshape(rows, -1)
    kt = k_all.T
    vt = v_all.T
    dat = da_s[...].reshape(rows, -1).T
    which = (
        lax.broadcasted_iota(jnp.int32, (rows, 128), 0) // BLOCK
        == lax.broadcasted_iota(jnp.int32, (rows, 128), 1)
    )
    onehot = jnp.where(which, 1.0, 0.0).astype(BF16)
    for p in range(pairs):
        lanes = slice(p * PAIR, (p + 1) * PAIR)
        kp_s[p, :, :PAIR] = k_all[:, lanes]
        kp_s[p, :, PAIR:] = onehot
        vp_s[p] = v_all[:, lanes]
        kt_s[p] = kt[lanes]
        vt_s[p] = vt[lanes]
        for a in range(n_blocks):
            dat_s[p, a] = dat[lanes, a * BLOCK : (a + 1) * BLOCK]
            r = slice((a % blocks) * BLOCK, (a % blocks + 1) * BLOCK)
            qb_s[p, a // blocks, a % blocks] = by_head(q_s[a // blocks, r, lanes])
            db_s[p, a // blocks, a % blocks] = by_head(da_s[a // blocks, r, lanes])

    def group(step, carry):
        p = step // 2
        g = step % 2
        for i in range(blocks):
            a = g * blocks + i
            q2 = qb_s[p, g, i]
            d2 = db_s[p, g, i]
            bias = jnp.broadcast_to(bs[g, i : i + 1, :], (2 * BLOCK, 128))
            scores = dot_nt(kp_s[p], jnp.concatenate([q2, bias], axis=1))
            top = jnp.max(scores, axis=0, keepdims=True)
            expo = jnp.exp(scores - top)
            prob = expo * (1.0 / jnp.sum(expo, axis=0, keepdims=True))
            weights = prob.astype(BF16)
            cols = slice(i * 2 * BLOCK, (i + 1) * 2 * BLOCK)
            w_s[:, cols] = weights
            mixed = dot_nn(vt_s[p], weights)
            att = jnp.concatenate([mixed[:HD, :BLOCK], mixed[HD:, BLOCK:]], axis=0).astype(BF16)
            prod = att.astype(F32) * dat_s[p, a].astype(F32)
            inner = jnp.concatenate(
                [
                    jnp.sum(prod[:HD], axis=0, keepdims=True),
                    jnp.sum(prod[HD:], axis=0, keepdims=True),
                ],
                axis=1,
            )
            at_s[p, a] = att
            att_s[p, g, i] = att.T
            d_scores = (prob * (dot_nt(vp_s[p], d2) - inner)).astype(BF16)
            ds_s[:, cols] = d_scores
            mixed = dot_nn(kt_s[p], d_scores)
            dqt = jnp.concatenate([mixed[:HD, :BLOCK], mixed[HD:, BLOCK:]], axis=0)
            dqt = (dqt * HD ** (-0.5)).astype(BF16)
            dqt_s[p, a] = dqt
            dq_s[p, g, i] = dqt.T
        dk_s[g, p] = dot_nn(ds_s[...], qb_s[p, g].reshape(-1, PAIR)).astype(BF16)
        dv_s[g, p] = dot_nn(w_s[...], db_s[p, g].reshape(-1, PAIR)).astype(BF16)
        return carry

    lax.fori_loop(0, 2 * pairs, group, 0)

    def whole(ref):
        return jnp.concatenate([ref[p].reshape(rows, PAIR) for p in range(pairs)], axis=1)

    h_all = hs[...].reshape(rows, -1)
    c_all = cs[...].reshape(rows, -1)
    ht = h_all.T
    ht_s[...] = ht

    def summed(ref):
        return jnp.concatenate(
            [(ref[0, p].astype(F32) + ref[1, p].astype(F32)).astype(BF16) for p in range(pairs)],
            axis=1,
        )

    attended = whole(att_s)
    d_query = whole(dq_s)
    d_key = summed(dk_s)
    d_value = summed(dv_s)
    result = (h_all.astype(F32) + dot_nn(attended, wo[...])).astype(BF16)
    osend[...] = result.reshape(osend.shape)
    back = (
        c_all.astype(F32)
        + dot_nt(d_query, wq[...])
        + dot_nt(d_key, wk[...])
        + dot_nt(d_value, wv[...])
    ).astype(BF16)
    gsend[...] = back.reshape(gsend.shape)
    sends = []
    for i, (src, dst) in enumerate(((osend, out), (gsend, grad))):
        copy = pltpu.make_async_remote_copy(
            src_ref=src.at[other], dst_ref=dst.at[e], send_sem=osem_s.at[i], recv_sem=osem_r.at[i],
            device_id={"elec": other}, device_id_type=pl.DeviceIdType.MESH,
        )
        copy.start()
        sends.append(copy)
    out[e] = osend[e]
    grad[e] = gsend[e]
    at = jnp.concatenate(
        [
            jnp.concatenate([at_s[p, a] for a in range(n_blocks)], axis=1)
            for p in range(pairs)
        ],
        axis=0,
    )
    parts = (
        dot_nn(ht_s[...], d_query), dot_nn(ht_s[...], d_key),
        dot_nn(ht_s[...], d_value), dot_nn(at, c_all),
    )
    width = hid.shape[2]
    per = 4 * width // 2
    for p in range(pairs):
        for t, part in enumerate(parts):
            g_s[p, t * width // per, pl.ds(t * width % per, width)] = part[:, p * PAIR : (p + 1) * PAIR]
        a_s[p] = g_s[p].astype(BF16)

    def transfers(stage, p):
        if stage == 0:
            todo = [(a_s.at[p, other], r0.at[p], core_id)]
        elif stage == 1:
            todo = [(b1.at[p, t], r1.at[p, r], spot_ids[r]) for r, t in enumerate(near)]
        elif stage == 2:
            todo = [(b2.at[p, t], r2.at[p, r], layer_ids[r]) for r, t in enumerate(layers)]
        elif stage == 3:
            todo = [(agz.at[p, plane], agz.at[p, plane], i) for i in layer_ids]
        elif stage == 4:
            todo = [(agxy.at[p, spot], agxy.at[p, spot], i) for i in spot_ids]
        else:
            todo = [(agxy.at[p], full.at[p, e], core_id)]
        return [
            pltpu.make_async_remote_copy(
                src_ref=src, dst_ref=dst, send_sem=ar_send.at[stage, p, r],
                recv_sem=ar_recv.at[stage, p, r], device_id=peer, device_id_type=mesh_ids,
            )
            for r, (src, dst, peer) in enumerate(todo)
        ]

    def begin(stage, p):
        for copy in transfers(stage, p):
            copy.start()

    def finish(stage, p):
        for copy in transfers(stage, p):
            copy.wait()
        if stage == 0:
            s1[p] = (g_s[p, e] + r0[p].astype(F32)).reshape(s1.shape[1:])
            b1[p] = s1[p].astype(BF16)
        elif stage == 1:
            total = s1[p, spot]
            for r in range(3):
                total = total + r1[p, r].astype(F32)
            s2[p] = total.reshape(s2.shape[1:])
            b2[p] = s2[p].astype(BF16)
        elif stage == 2:
            total = s2[p, plane]
            for r in range(planes - 1):
                total = total + r2[p, r].astype(F32)
            agz[p, plane] = (total * (1.0 / (2 * lax.axis_size("walk")))).astype(BF16)
        elif stage == 3:
            agxy[p, spot] = agz[p]
        elif stage == 4:
            full[p, e] = agxy[p]

    for p in range(pairs):
        begin(0, p)
    for stage in range(6):
        for p in range(pairs):
            finish(stage, p)
            if stage < 5:
                begin(stage + 1, p)
    for copy in sends:
        copy.wait()


def write_kernel(out, grad, full, out_h, grad_h, gq_h, gk_h, gv_h, go_h, gq, gk, gv, go, sem):
    copies = [pltpu.make_async_copy(out, out_h, sem.at[0]), pltpu.make_async_copy(grad, grad_h, sem.at[1])]
    for copy in copies:
        copy.start()
    width = gq.shape[0]
    pairs = full.shape[0]
    for t, (dst, dst_h) in enumerate(((gq, gq_h), (gk, gk_h), (gv, gv_h), (go, go_h))):
        for p in range(pairs):
            rows = full[p].reshape(4 * width, PAIR)[t * width : (t + 1) * width]
            dst[:, p * PAIR : (p + 1) * PAIR] = rows.astype(F32)
        copies.append(pltpu.make_async_copy(dst, dst_h, sem.at[2 + t]))
        copies[-1].start()
    for copy in copies:
        copy.wait()


def pair_body(hidden, w_query, w_key, w_value, w_out, neighbours, counts, cotangent):
    half, width = hidden.shape[1:]
    blocks = half // BLOCK
    rows, pairs, n_blocks = 2 * half, width // PAIR, 2 * blocks
    vmem = pl.BlockSpec(memory_space=pltpu.VMEM)
    smem = pl.BlockSpec(memory_space=pltpu.SMEM)
    hbm = pl.BlockSpec(memory_space=pltpu.HBM)
    planes = lax.axis_size("walk") // 4
    peers = max(3, planes - 1)
    per = 4 * width // 2
    fine = per // 4 // planes
    both = (2, half, width)
    by_pair = (pairs, 2, blocks, BLOCK, PAIR)
    by_pair2 = (pairs, 2, blocks, 2 * BLOCK, PAIR)

    def buf(*shape, dtype=BF16):
        return pltpu.VMEM(shape, dtype)

    out, grad, full = pl.pallas_call(
        walker_kernel,
        out_shape=(
            jax.ShapeDtypeStruct(hidden.shape, BF16),
            jax.ShapeDtypeStruct(hidden.shape, BF16),
            jax.ShapeDtypeStruct((pairs, 2, 4, planes, fine, PAIR), BF16),
        ),
        in_specs=[smem, smem] + [hbm] * 6,
        out_specs=(vmem, vmem, vmem),
        scratch_shapes=[
            buf(width, width), buf(width, width), buf(width, width), buf(width, width),
            buf(*both), buf(*both), buf(2, 16, 128), buf(2, 16, 128),
            buf(*both), buf(*both), buf(*both), buf(*both),
            buf(pairs, PAIR, rows), buf(pairs, PAIR, rows), buf(pairs, n_blocks, PAIR, BLOCK),
            buf(pairs, n_blocks, PAIR, BLOCK), buf(*by_pair),
            buf(pairs, n_blocks, PAIR, BLOCK), buf(*by_pair),
            buf(rows, blocks * 2 * BLOCK), buf(rows, blocks * 2 * BLOCK),
            buf(*by_pair2), buf(*by_pair2),
            buf(pairs, rows, 2 * PAIR), buf(pairs, rows, PAIR),
            buf(2, pairs, rows, PAIR), buf(2, pairs, rows, PAIR),
            buf(width, rows), buf(*both), buf(*both),
            buf(pairs, 2, per, PAIR, dtype=F32), buf(pairs, 2, per, PAIR), buf(pairs, per, PAIR),
            buf(pairs, 4, per // 4, PAIR, dtype=F32), buf(pairs, 4, per // 4, PAIR),
            buf(pairs, 3, per // 4, PAIR),
            buf(pairs, planes, fine, PAIR, dtype=F32), buf(pairs, planes, fine, PAIR),
            buf(pairs, planes - 1, fine, PAIR),
            buf(pairs, planes, fine, PAIR), buf(pairs, 4, planes, fine, PAIR),
            pltpu.SemaphoreType.DMA((3,)), pltpu.SemaphoreType.DMA((3,)),
            pltpu.SemaphoreType.DMA((6,)),
            pltpu.SemaphoreType.DMA((2,)), pltpu.SemaphoreType.DMA((2,)),
            pltpu.SemaphoreType.DMA((6, pairs, peers)), pltpu.SemaphoreType.DMA((6, pairs, peers)),
        ],
        compiler_params=pltpu.CompilerParams(
            collective_id=0, has_side_effects=True, vmem_limit_bytes=48 * 1024 * 1024
        ),
    )(neighbours, counts, hidden, cotangent, w_query, w_key, w_value, w_out)
    grads = jax.ShapeDtypeStruct((width, width), F32)
    return pl.pallas_call(
        write_kernel,
        out_shape=(
            jax.ShapeDtypeStruct(hidden.shape, BF16), jax.ShapeDtypeStruct(hidden.shape, BF16),
            grads, grads, grads, grads,
        ),
        in_specs=[pl.BlockSpec(memory_space=pl.ANY)] * 2 + [vmem],
        out_specs=(hbm,) * 6,
        scratch_shapes=[buf(width, width, dtype=F32)] * 4 + [pltpu.SemaphoreType.DMA((6,))],
    )(out, grad, full)


def any_body(hidden, *rest):
    blocks = rest[4].shape[1]
    fits = hidden.shape[0] == 2 and 2 * blocks <= 128 and blocks <= 16
    if fits and lax.axis_size("elec") == 2 and lax.axis_size("walk") in (8, 16):
        return pair_body(hidden, *rest)
    return body(hidden, *rest)


def solution(mesh):
    placed = (
        P("walk", "elec", None),
        P(),
        P(),
        P(),
        P(),
        P("walk", "elec", None),
        P("walk", "elec"),
        P("walk", "elec", None),
    )
    return jax.shard_map(
        any_body,
        mesh=mesh,
        in_specs=placed,
        out_specs=(P("walk", "elec", None), P("walk", "elec", None), P(), P(), P(), P()),
        check_vma=False,
    )
```

```python
import jax
import jax.numpy as jnp
from jax import lax
from jax.experimental import pallas as pl
from jax.experimental.pallas import tpu as pltpu
from jax.sharding import PartitionSpec as P

HD = 64
BLOCK = 128


NEG_FILL = -1e30


def split_heads(array, head_count):
    return array.reshape(array.shape[:-1] + (head_count, array.shape[-1] // head_count))


def masked_scores(query_blk, key_slots, valid_keys, head_count, scaling):
    scores = (
        jnp.einsum(
            "bhd,khd->hbk",
            split_heads(query_blk, head_count),
            split_heads(key_slots, head_count),
            preferred_element_type=jnp.float32,
        )
        * scaling
    )
    return jnp.where(valid_keys[None, None, :], scores, NEG_FILL)


def body(hidden, w_query, w_key, w_value, w_out, neighbours, counts, cotangent):
    walk_dev, local_rows, model_width = hidden.shape
    blocks = neighbours.shape[1]
    slot_count = neighbours.shape[2]
    head_count = model_width // HD
    scaling = HD ** (-0.5)
    all_rows = hidden.reshape(-1, model_width)
    joined = jnp.concatenate([w_query, w_key, w_value], axis=1)
    projected = jnp.dot(all_rows, joined, preferred_element_type=jnp.float32).astype(jnp.bfloat16)
    query_rows = projected[:, :model_width]
    key_blocks = projected[:, model_width : 2 * model_width].reshape(
        walk_dev, blocks, BLOCK, model_width
    )
    value_blocks = projected[:, 2 * model_width :].reshape(walk_dev, blocks, BLOCK, model_width)
    cot_rows = cotangent.reshape(-1, model_width)
    d_attended = jnp.dot(cot_rows, w_out.T, preferred_element_type=jnp.float32).astype(jnp.bfloat16)
    key_store, value_store = (
        lax.all_gather(key_blocks, "elec", axis=1, tiled=True),
        lax.all_gather(value_blocks, "elec", axis=1, tiled=True),
    )
    stored = key_store.shape[1]
    walker_base = stored * jnp.arange(walk_dev, dtype=jnp.int32)[:, None, None]
    flat_slots = (neighbours + walker_base).reshape(-1, slot_count)
    key_flat = key_store.reshape(-1, BLOCK, model_width)
    value_flat = value_store.reshape(-1, BLOCK, model_width)
    query_items = query_rows.reshape(-1, BLOCK, model_width)
    count_items = counts.reshape(-1)
    grad_items = d_attended.reshape(-1, BLOCK, model_width)

    def slot_rows(flat_row, live_count):
        key_slots = jnp.take(key_flat, flat_row, axis=0).reshape(slot_count * BLOCK, model_width)
        value_slots = jnp.take(value_flat, flat_row, axis=0).reshape(
            slot_count * BLOCK, model_width
        )
        valid_keys = jnp.repeat(jnp.arange(slot_count, dtype=jnp.int32) < live_count, BLOCK)
        return (key_slots, value_slots, valid_keys)

    def forward_item(inputs):
        query_blk, flat_row, live_count = inputs
        key_slots, value_slots, valid_keys = slot_rows(flat_row, live_count)
        scores = masked_scores(query_blk, key_slots, valid_keys, head_count, scaling)
        row_max = jnp.max(scores, axis=-1, keepdims=True)
        log_total = row_max + jnp.log(jnp.sum(jnp.exp(scores - row_max), axis=-1, keepdims=True))
        weights = jnp.exp(scores - log_total).astype(jnp.bfloat16)
        attended = jnp.einsum(
            "hbk,khd->bhd",
            weights,
            split_heads(value_slots, head_count),
            preferred_element_type=jnp.float32,
        )
        return (attended.astype(jnp.bfloat16).reshape(BLOCK, model_width), log_total)

    attended_items, log_items = lax.map(forward_item, (query_items, flat_slots, count_items))
    attended_rows = attended_items.reshape(-1, model_width)
    output = (
        all_rows.astype(jnp.float32)
        + jnp.dot(attended_rows, w_out, preferred_element_type=jnp.float32)
    ).astype(jnp.bfloat16)
    walkers_all = walk_dev * lax.axis_size("walk")
    grad_out = jnp.dot(attended_rows.T, cot_rows, preferred_element_type=jnp.float32) / walkers_all

    def backward_item(inputs):
        query_blk, flat_row, live_count, attended_blk, log_total, grad_blk = inputs
        key_slots, value_slots, valid_keys = slot_rows(flat_row, live_count)
        scores = masked_scores(query_blk, key_slots, valid_keys, head_count, scaling)
        probabilities = jnp.exp(scores - log_total)
        weights = probabilities.astype(jnp.bfloat16)
        grad_heads = split_heads(grad_blk, head_count)
        d_weights = jnp.einsum(
            "bhd,khd->hbk",
            grad_heads,
            split_heads(value_slots, head_count),
            preferred_element_type=jnp.float32,
        )
        inner_sum = jnp.sum(
            grad_heads.astype(jnp.float32)
            * split_heads(attended_blk, head_count).astype(jnp.float32),
            axis=-1,
        ).T
        score_grad = (probabilities * (d_weights - inner_sum[..., None])).astype(jnp.bfloat16)
        d_query = (
            jnp.einsum(
                "hbk,khd->bhd",
                score_grad,
                split_heads(key_slots, head_count),
                preferred_element_type=jnp.float32,
            )
            * scaling
        )
        key_terms = (
            jnp.einsum(
                "hbk,bhd->khd",
                score_grad,
                split_heads(query_blk, head_count),
                preferred_element_type=jnp.float32,
            )
            * scaling
        )
        value_terms = jnp.einsum(
            "hbk,bhd->khd", weights, grad_heads, preferred_element_type=jnp.float32
        )
        return (
            d_query.astype(jnp.bfloat16).reshape(BLOCK, model_width),
            key_terms.reshape(-1, model_width),
            value_terms.reshape(-1, model_width),
        )

    query_grad_items, key_terms, value_terms = lax.map(
        backward_item, (query_items, flat_slots, count_items, attended_items, log_items, grad_items)
    )
    onehot = (
        neighbours.reshape(walk_dev, blocks * slot_count)[..., None]
        == jnp.arange(stored, dtype=jnp.int32)[None, None, :]
    ).astype(jnp.float32)

    def place(contribution):
        grouped = contribution.reshape(walk_dev, blocks * slot_count, BLOCK * model_width)
        placed = jnp.einsum("wsn,wsx->wnx", onehot, grouped, precision=lax.Precision.HIGHEST)
        return placed.reshape(walk_dev, stored, BLOCK, model_width).astype(jnp.bfloat16)

    key_round = place(key_terms)
    value_round = place(value_terms)
    key_wide = lax.optimization_barrier(key_round).astype(jnp.float32)
    value_wide = lax.optimization_barrier(value_round).astype(jnp.float32)
    key_sum, value_sum = (
        lax.psum_scatter(
            key_wide.astype(jnp.bfloat16), "elec", scatter_dimension=1, tiled=True
        ).astype(jnp.float32),
        lax.psum_scatter(
            value_wide.astype(jnp.bfloat16), "elec", scatter_dimension=1, tiled=True
        ).astype(jnp.float32),
    )
    key_grad_rows = key_sum.astype(jnp.bfloat16).reshape(-1, model_width)
    value_grad_rows = value_sum.astype(jnp.bfloat16).reshape(-1, model_width)
    query_grad_rows = query_grad_items.reshape(-1, model_width)
    grad_hidden = cot_rows.astype(jnp.float32) + jnp.dot(
        query_grad_rows, w_query.T, preferred_element_type=jnp.float32
    )
    grad_hidden = grad_hidden + jnp.dot(key_grad_rows, w_key.T, preferred_element_type=jnp.float32)
    grad_hidden = grad_hidden + jnp.dot(
        value_grad_rows, w_value.T, preferred_element_type=jnp.float32
    )
    grad_hidden = grad_hidden.astype(jnp.bfloat16).reshape(hidden.shape)
    grad_query = (
        jnp.dot(all_rows.T, query_grad_rows, preferred_element_type=jnp.float32) / walkers_all
    )
    grad_key = jnp.dot(all_rows.T, key_grad_rows, preferred_element_type=jnp.float32) / walkers_all
    grad_value = (
        jnp.dot(all_rows.T, value_grad_rows, preferred_element_type=jnp.float32) / walkers_all
    )
    grad_query, grad_key, grad_value, grad_out = lax.psum(
        (grad_query, grad_key, grad_value, grad_out), ("walk", "elec")
    )
    return (output.reshape(hidden.shape), grad_hidden, grad_query, grad_key, grad_value, grad_out)


F32 = jnp.float32
BF16 = jnp.bfloat16
PAIR = 2 * HD


def dot_nn(a, b):
    return lax.dot_general(a, b, (((1,), (0,)), ((), ())), preferred_element_type=F32)


def dot_nt(a, b):
    return lax.dot_general(a, b, (((1,), (1,)), ((), ())), preferred_element_type=F32)


def by_head(block):
    lane = lax.broadcasted_iota(jnp.int32, block.shape, 1)
    zero = jnp.zeros_like(block)
    return jnp.concatenate(
        [jnp.where(lane < HD, block, zero), jnp.where(lane < HD, zero, block)], axis=0
    )


def walker_kernel(
    nbr, cnt, hid, cot, wq_h, wk_h, wv_h, wo_h, out, grad, full,
    wq, wk, wv, wo, hs, cs, bs, bsend, q_s, k_s, v_s, da_s, kt_s, vt_s, dat_s,
    at_s, att_s, dqt_s, dq_s, w_s, ds_s, qb_s, db_s, kp_s, vp_s, dk_s, dv_s, ht_s, osend, gsend,
    g_s, a_s, r0, s1, b1, r1, s2, b2, r2, agz, agxy,
    send_sem, recv_sem, local_sem, osem_s, osem_r, ar_send, ar_recv,
):
    e = lax.axis_index("elec")
    other = 1 - e
    blocks = hid.shape[1] // BLOCK
    slots = nbr.shape[2]
    n_blocks = 2 * blocks
    half = hid.shape[1]
    rows = 2 * half
    pairs = hid.shape[2] // PAIR

    walk = lax.axis_index("walk")
    planes = lax.axis_size("walk") // 4
    plane, spot = walk // 4, walk % 4
    sx, sy = spot % 2, spot // 2
    near = [((sy + r // 2) % 2) * 2 + (sx + r % 2) % 2 for r in range(1, 4)]
    layers = [(plane + r) % planes for r in range(1, planes)]
    spot_ids = [{"walk": plane * 4 + t, "elec": e} for t in near]
    layer_ids = [{"walk": t * 4 + spot, "elec": e} for t in layers]
    core_id = {"walk": walk, "elec": other}
    mesh_ids = pl.DeviceIdType.MESH

    barrier = pltpu.get_barrier_semaphore()
    for peer in [core_id] + spot_ids + layer_ids:
        pl.semaphore_signal(barrier, inc=1, device_id=peer, device_id_type=mesh_ids)

    local = [
        pltpu.make_async_copy(src, dst, local_sem.at[i])
        for i, (src, dst) in enumerate(
            (
                (hid.at[e], hs.at[e]), (wq_h, wq), (wk_h, wk), (wv_h, wv),
                (cot.at[e], cs.at[e]), (wo_h, wo),
            )
        )
    ]
    for copy in local:
        copy.start()

    lane = lax.broadcasted_iota(jnp.int32, (16, 128), 1)
    sub = lax.broadcasted_iota(jnp.int32, (16, 128), 0)
    for w in range(2):
        bias = jnp.full((16, 128), NEG_FILL, F32)
        for a in range(blocks):
            for j in range(slots):
                live = jnp.where(j < cnt[w, a], nbr[w, a, j], -1)
                bias = jnp.where((sub == a) & (lane == live), 0.0, bias)
        bsend[w] = bias.astype(BF16)

    pl.semaphore_wait(barrier, 3 + planes)
    sends = []
    for i, (src, dst) in enumerate(((hid, hs), (cot, cs), (bsend, bs))):
        copy = pltpu.make_async_remote_copy(
            src_ref=src.at[other], dst_ref=dst.at[e], send_sem=send_sem.at[i], recv_sem=recv_sem.at[i],
            device_id={"elec": other}, device_id_type=pl.DeviceIdType.MESH,
        )
        copy.start()
        sends.append(copy)

    bs[e] = bsend[e]
    for copy in local:
        copy.wait()

    def project(h):
        rows_h = hs[h]
        q_s[h] = (dot_nn(rows_h, wq[...]).astype(BF16).astype(F32) * HD ** (-0.5)).astype(BF16)
        k_s[h] = dot_nn(rows_h, wk[...]).astype(BF16)
        v_s[h] = dot_nn(rows_h, wv[...]).astype(BF16)
        da_s[h] = dot_nt(cs[h], wo[...]).astype(BF16)

    project(e)
    for copy in sends:
        copy.wait()
    project(other)

    k_all = k_s[...].reshape(rows, -1)
    v_all = v_s[...].reshape(rows, -1)
    kt = k_all.T
    vt = v_all.T
    dat = da_s[...].reshape(rows, -1).T
    which = (
        lax.broadcasted_iota(jnp.int32, (rows, 128), 0) // BLOCK
        == lax.broadcasted_iota(jnp.int32, (rows, 128), 1)
    )
    onehot = jnp.where(which, 1.0, 0.0).astype(BF16)
    for p in range(pairs):
        lanes = slice(p * PAIR, (p + 1) * PAIR)
        kp_s[p, :, :PAIR] = k_all[:, lanes]
        kp_s[p, :, PAIR:] = onehot
        vp_s[p] = v_all[:, lanes]
        kt_s[p] = kt[lanes]
        vt_s[p] = vt[lanes]
        for a in range(n_blocks):
            dat_s[p, a] = dat[lanes, a * BLOCK : (a + 1) * BLOCK]
            r = slice((a % blocks) * BLOCK, (a % blocks + 1) * BLOCK)
            qb_s[p, a // blocks, a % blocks] = by_head(q_s[a // blocks, r, lanes])
            db_s[p, a // blocks, a % blocks] = by_head(da_s[a // blocks, r, lanes])

    ht_s[...] = hs[...].reshape(rows, -1).T

    def group(p, g, hooks=None):
        for i in range(blocks):
            a = g * blocks + i
            q2 = qb_s[p, g, i]
            d2 = db_s[p, g, i]
            bias = jnp.broadcast_to(bs[g, i : i + 1, :], (2 * BLOCK, 128))
            scores = dot_nt(kp_s[p], jnp.concatenate([q2, bias], axis=1))
            top = jnp.max(scores, axis=0, keepdims=True)
            expo = jnp.exp(scores - top)
            prob = expo * (1.0 / jnp.sum(expo, axis=0, keepdims=True))
            weights = prob.astype(BF16)
            cols = slice(i * 2 * BLOCK, (i + 1) * 2 * BLOCK)
            w_s[:, cols] = weights
            mixed = dot_nn(vt_s[p], weights)
            att = jnp.concatenate([mixed[:HD, :BLOCK], mixed[HD:, BLOCK:]], axis=0).astype(BF16)
            prod = att.astype(F32) * dat_s[p, a].astype(F32)
            inner = jnp.concatenate(
                [
                    jnp.sum(prod[:HD], axis=0, keepdims=True),
                    jnp.sum(prod[HD:], axis=0, keepdims=True),
                ],
                axis=1,
            )
            at_s[p, a] = att
            att_s[p, g, i] = att.T
            d_scores = (prob * (dot_nt(vp_s[p], d2) - inner)).astype(BF16)
            ds_s[:, cols] = d_scores
            mixed = dot_nn(kt_s[p], d_scores)
            dqt = jnp.concatenate([mixed[:HD, :BLOCK], mixed[HD:, BLOCK:]], axis=0)
            dqt = (dqt * HD ** (-0.5)).astype(BF16)
            dqt_s[p, a] = dqt
            dq_s[p, g, i] = dqt.T
            if hooks and hooks[i]:
                hooks[i]()
        dk_s[g, p] = dot_nn(ds_s[...], qb_s[p, g].reshape(-1, PAIR)).astype(BF16)
        dv_s[g, p] = dot_nn(w_s[...], db_s[p, g].reshape(-1, PAIR)).astype(BF16)
    width = hid.shape[2]

    def summed(ref, p):
        return (ref[0, p].astype(F32) + ref[1, p].astype(F32)).astype(BF16)

    def weight_parts(p):
        lower = g_s.at[p, 0]
        upper = g_s.at[p, 1]
        lower[:width] = dot_nn(ht_s[...], dq_s[p].reshape(rows, PAIR))
        lower[width:] = dot_nn(ht_s[...], summed(dk_s, p))
        upper[:width] = dot_nn(ht_s[...], summed(dv_s, p))
        at = jnp.concatenate([at_s[p, a] for a in range(n_blocks)], axis=1)
        part = dot_nn(at, cs[...].reshape(rows, -1))
        for c in range(pairs):
            upper[pl.ds(width + c * PAIR, PAIR)] = part[:, c * PAIR : (c + 1) * PAIR]
        a_s[p] = g_s[p, other].astype(BF16)

    def transfers(stage, p):
        if stage == 0:
            todo = [(a_s.at[p], r0.at[p], core_id)]
        elif stage == 1:
            todo = [(b1.at[p, t], r1.at[p, r], spot_ids[r]) for r, t in enumerate(near)]
        elif stage == 2:
            todo = [(b2.at[p, t], r2.at[p, r], layer_ids[r]) for r, t in enumerate(layers)]
        elif stage == 3:
            todo = [(agz.at[p, plane], agz.at[p, plane], i) for i in layer_ids]
        elif stage == 4:
            todo = [(agxy.at[p, spot], agxy.at[p, spot], i) for i in spot_ids]
        else:
            todo = [(agxy.at[p], full.at[p, e], core_id)]
        return [
            pltpu.make_async_remote_copy(
                src_ref=src, dst_ref=dst, send_sem=ar_send.at[stage, p, r],
                recv_sem=ar_recv.at[stage, p, r], device_id=peer, device_id_type=mesh_ids,
            )
            for r, (src, dst, peer) in enumerate(todo)
        ]

    def begin(stage, p):
        for copy in transfers(stage, p):
            copy.start()

    def finish(stage, p):
        for copy in transfers(stage, p):
            copy.wait()
        if stage == 0:
            s1[p] = (g_s[p, e] + r0[p].astype(F32)).reshape(s1.shape[1:])
            b1[p] = s1[p].astype(BF16)
        elif stage == 1:
            total = s1[p, spot]
            for r in range(3):
                total = total + r1[p, r].astype(F32)
            s2[p] = total.reshape(s2.shape[1:])
            b2[p] = s2[p].astype(BF16)
        elif stage == 2:
            total = s2[p, plane]
            for r in range(planes - 1):
                total = total + r2[p, r].astype(F32)
            agz[p, plane] = (total * (1.0 / (2 * lax.axis_size("walk")))).astype(BF16)
        elif stage == 3:
            agxy[p, spot] = agz[p]
        elif stage == 4:
            full[p, e] = agxy[p]


    def advance(stage, p):
        finish(stage, p)
        begin(stage + 1, p)

    def first_pair(g, carry):
        group(0, g)
        return carry

    lax.fori_loop(0, 2, first_pair, 0)
    weight_parts(0)
    begin(0, 0)
    group(1, 0, [None, lambda: advance(0, 0), None])
    group(1, 1, [lambda: advance(1, 0), None, lambda: advance(2, 0)])
    weight_parts(1)
    begin(0, 1)

    def whole(ref):
        return jnp.concatenate([ref[p].reshape(rows, PAIR) for p in range(pairs)], axis=1)

    def give(i, src, dst):
        copy = pltpu.make_async_remote_copy(
            src_ref=src.at[other], dst_ref=dst.at[e], send_sem=osem_s.at[i], recv_sem=osem_r.at[i],
            device_id=core_id, device_id_type=mesh_ids,
        )
        copy.start()
        dst[e] = src[e]
        return copy

    result = (hs[...].reshape(rows, -1).astype(F32) + dot_nn(whole(att_s), wo[...])).astype(BF16)
    osend[...] = result.reshape(osend.shape)
    advance(0, 1)
    advance(3, 0)
    sends = [give(0, osend, out)]
    d_key = jnp.concatenate([summed(dk_s, p) for p in range(pairs)], axis=1)
    d_value = jnp.concatenate([summed(dv_s, p) for p in range(pairs)], axis=1)
    back = (
        cs[...].reshape(rows, -1).astype(F32)
        + dot_nt(whole(dq_s), wq[...])
        + dot_nt(d_key, wk[...])
        + dot_nt(d_value, wv[...])
    ).astype(BF16)
    gsend[...] = back.reshape(gsend.shape)
    advance(1, 1)
    sends.append(give(1, gsend, grad))
    advance(4, 0)
    advance(2, 1)
    advance(3, 1)
    finish(5, 0)
    advance(4, 1)
    for copy in sends:
        copy.wait()
    finish(5, 1)


def write_kernel(out, grad, full, out_h, grad_h, gq_h, gk_h, gv_h, go_h, gq, gk, gv, go, sem):
    copies = [pltpu.make_async_copy(out, out_h, sem.at[0]), pltpu.make_async_copy(grad, grad_h, sem.at[1])]
    for copy in copies:
        copy.start()
    width = gq.shape[0]
    pairs = full.shape[0]
    for t, (dst, dst_h) in enumerate(((gq, gq_h), (gk, gk_h), (gv, gv_h), (go, go_h))):
        for p in range(pairs):
            rows = full[p].reshape(4 * width, PAIR)[t * width : (t + 1) * width].astype(F32)
            if t < 3:
                dst[:, p * PAIR : (p + 1) * PAIR] = rows
            else:
                for c in range(pairs):
                    dst[p * PAIR : (p + 1) * PAIR, c * PAIR : (c + 1) * PAIR] = rows[c * PAIR : (c + 1) * PAIR]
        copies.append(pltpu.make_async_copy(dst, dst_h, sem.at[2 + t]))
        copies[-1].start()
    for copy in copies:
        copy.wait()


def pair_body(hidden, w_query, w_key, w_value, w_out, neighbours, counts, cotangent):
    half, width = hidden.shape[1:]
    blocks = half // BLOCK
    rows, pairs, n_blocks = 2 * half, width // PAIR, 2 * blocks
    vmem = pl.BlockSpec(memory_space=pltpu.VMEM)
    smem = pl.BlockSpec(memory_space=pltpu.SMEM)
    hbm = pl.BlockSpec(memory_space=pltpu.HBM)
    planes = lax.axis_size("walk") // 4
    peers = max(3, planes - 1)
    per = 4 * width // 2
    fine = per // 4 // planes
    both = (2, half, width)
    by_pair = (pairs, 2, blocks, BLOCK, PAIR)
    by_pair2 = (pairs, 2, blocks, 2 * BLOCK, PAIR)

    def buf(*shape, dtype=BF16):
        return pltpu.VMEM(shape, dtype)

    out, grad, full = pl.pallas_call(
        walker_kernel,
        out_shape=(
            jax.ShapeDtypeStruct(hidden.shape, BF16),
            jax.ShapeDtypeStruct(hidden.shape, BF16),
            jax.ShapeDtypeStruct((pairs, 2, 4, planes, fine, PAIR), BF16),
        ),
        in_specs=[smem, smem] + [hbm] * 6,
        out_specs=(vmem, vmem, vmem),
        scratch_shapes=[
            buf(width, width), buf(width, width), buf(width, width), buf(width, width),
            buf(*both), buf(*both), buf(2, 16, 128), buf(2, 16, 128),
            buf(*both), buf(*both), buf(*both), buf(*both),
            buf(pairs, PAIR, rows), buf(pairs, PAIR, rows), buf(pairs, n_blocks, PAIR, BLOCK),
            buf(pairs, n_blocks, PAIR, BLOCK), buf(*by_pair),
            buf(pairs, n_blocks, PAIR, BLOCK), buf(*by_pair),
            buf(rows, blocks * 2 * BLOCK), buf(rows, blocks * 2 * BLOCK),
            buf(*by_pair2), buf(*by_pair2),
            buf(pairs, rows, 2 * PAIR), buf(pairs, rows, PAIR),
            buf(2, pairs, rows, PAIR), buf(2, pairs, rows, PAIR),
            buf(width, rows), buf(*both), buf(*both),
            buf(pairs, 2, per, PAIR, dtype=F32), buf(pairs, per, PAIR), buf(pairs, per, PAIR),
            buf(pairs, 4, per // 4, PAIR, dtype=F32), buf(pairs, 4, per // 4, PAIR),
            buf(pairs, 3, per // 4, PAIR),
            buf(pairs, planes, fine, PAIR, dtype=F32), buf(pairs, planes, fine, PAIR),
            buf(pairs, planes - 1, fine, PAIR),
            buf(pairs, planes, fine, PAIR), buf(pairs, 4, planes, fine, PAIR),
            pltpu.SemaphoreType.DMA((3,)), pltpu.SemaphoreType.DMA((3,)),
            pltpu.SemaphoreType.DMA((6,)),
            pltpu.SemaphoreType.DMA((2,)), pltpu.SemaphoreType.DMA((2,)),
            pltpu.SemaphoreType.DMA((6, pairs, peers)), pltpu.SemaphoreType.DMA((6, pairs, peers)),
        ],
        compiler_params=pltpu.CompilerParams(
            collective_id=0, has_side_effects=True, vmem_limit_bytes=62 * 1024 * 1024 + 768 * 1024
        ),
    )(neighbours, counts, hidden, cotangent, w_query, w_key, w_value, w_out)
    grads = jax.ShapeDtypeStruct((width, width), F32)
    return pl.pallas_call(
        write_kernel,
        out_shape=(
            jax.ShapeDtypeStruct(hidden.shape, BF16), jax.ShapeDtypeStruct(hidden.shape, BF16),
            grads, grads, grads, grads,
        ),
        in_specs=[vmem] * 3,
        out_specs=(hbm,) * 6,
        scratch_shapes=[buf(width, width, dtype=F32)] * 4 + [pltpu.SemaphoreType.DMA((6,))],
    )(out, grad, full)


def any_body(hidden, *rest):
    blocks = rest[4].shape[1]
    fits = hidden.shape[0] == 2 and hidden.shape[2] == 2 * PAIR and 2 * blocks <= 128 and blocks <= 16
    if fits and lax.axis_size("elec") == 2 and lax.axis_size("walk") in (8, 16):
        return pair_body(hidden, *rest)
    return body(hidden, *rest)


def solution(mesh):
    placed = (
        P("walk", "elec", None),
        P(),
        P(),
        P(),
        P(),
        P("walk", "elec", None),
        P("walk", "elec"),
        P("walk", "elec", None),
    )
    return jax.shard_map(
        any_body,
        mesh=mesh,
        in_specs=placed,
        out_specs=(P("walk", "elec", None), P("walk", "elec", None), P(), P(), P(), P()),
        check_vma=False,
    )
```

```python
import jax
import jax.numpy as jnp
from jax import lax
from jax.experimental import pallas as pl
from jax.experimental.pallas import tpu as pltpu
from jax.sharding import PartitionSpec as P

HD = 64
BLOCK = 128


NEG_FILL = -1e30


def split_heads(array, head_count):
    return array.reshape(array.shape[:-1] + (head_count, array.shape[-1] // head_count))


def masked_scores(query_blk, key_slots, valid_keys, head_count, scaling):
    scores = (
        jnp.einsum(
            "bhd,khd->hbk",
            split_heads(query_blk, head_count),
            split_heads(key_slots, head_count),
            preferred_element_type=jnp.float32,
        )
        * scaling
    )
    return jnp.where(valid_keys[None, None, :], scores, NEG_FILL)


def body(hidden, w_query, w_key, w_value, w_out, neighbours, counts, cotangent):
    walk_dev, local_rows, model_width = hidden.shape
    blocks = neighbours.shape[1]
    slot_count = neighbours.shape[2]
    head_count = model_width // HD
    scaling = HD ** (-0.5)
    all_rows = hidden.reshape(-1, model_width)
    joined = jnp.concatenate([w_query, w_key, w_value], axis=1)
    projected = jnp.dot(all_rows, joined, preferred_element_type=jnp.float32).astype(jnp.bfloat16)
    query_rows = projected[:, :model_width]
    key_blocks = projected[:, model_width : 2 * model_width].reshape(
        walk_dev, blocks, BLOCK, model_width
    )
    value_blocks = projected[:, 2 * model_width :].reshape(walk_dev, blocks, BLOCK, model_width)
    cot_rows = cotangent.reshape(-1, model_width)
    d_attended = jnp.dot(cot_rows, w_out.T, preferred_element_type=jnp.float32).astype(jnp.bfloat16)
    key_store, value_store = (
        lax.all_gather(key_blocks, "elec", axis=1, tiled=True),
        lax.all_gather(value_blocks, "elec", axis=1, tiled=True),
    )
    stored = key_store.shape[1]
    walker_base = stored * jnp.arange(walk_dev, dtype=jnp.int32)[:, None, None]
    flat_slots = (neighbours + walker_base).reshape(-1, slot_count)
    key_flat = key_store.reshape(-1, BLOCK, model_width)
    value_flat = value_store.reshape(-1, BLOCK, model_width)
    query_items = query_rows.reshape(-1, BLOCK, model_width)
    count_items = counts.reshape(-1)
    grad_items = d_attended.reshape(-1, BLOCK, model_width)

    def slot_rows(flat_row, live_count):
        key_slots = jnp.take(key_flat, flat_row, axis=0).reshape(slot_count * BLOCK, model_width)
        value_slots = jnp.take(value_flat, flat_row, axis=0).reshape(
            slot_count * BLOCK, model_width
        )
        valid_keys = jnp.repeat(jnp.arange(slot_count, dtype=jnp.int32) < live_count, BLOCK)
        return (key_slots, value_slots, valid_keys)

    def forward_item(inputs):
        query_blk, flat_row, live_count = inputs
        key_slots, value_slots, valid_keys = slot_rows(flat_row, live_count)
        scores = masked_scores(query_blk, key_slots, valid_keys, head_count, scaling)
        row_max = jnp.max(scores, axis=-1, keepdims=True)
        log_total = row_max + jnp.log(jnp.sum(jnp.exp(scores - row_max), axis=-1, keepdims=True))
        weights = jnp.exp(scores - log_total).astype(jnp.bfloat16)
        attended = jnp.einsum(
            "hbk,khd->bhd",
            weights,
            split_heads(value_slots, head_count),
            preferred_element_type=jnp.float32,
        )
        return (attended.astype(jnp.bfloat16).reshape(BLOCK, model_width), log_total)

    attended_items, log_items = lax.map(forward_item, (query_items, flat_slots, count_items))
    attended_rows = attended_items.reshape(-1, model_width)
    output = (
        all_rows.astype(jnp.float32)
        + jnp.dot(attended_rows, w_out, preferred_element_type=jnp.float32)
    ).astype(jnp.bfloat16)
    walkers_all = walk_dev * lax.axis_size("walk")
    grad_out = jnp.dot(attended_rows.T, cot_rows, preferred_element_type=jnp.float32) / walkers_all

    def backward_item(inputs):
        query_blk, flat_row, live_count, attended_blk, log_total, grad_blk = inputs
        key_slots, value_slots, valid_keys = slot_rows(flat_row, live_count)
        scores = masked_scores(query_blk, key_slots, valid_keys, head_count, scaling)
        probabilities = jnp.exp(scores - log_total)
        weights = probabilities.astype(jnp.bfloat16)
        grad_heads = split_heads(grad_blk, head_count)
        d_weights = jnp.einsum(
            "bhd,khd->hbk",
            grad_heads,
            split_heads(value_slots, head_count),
            preferred_element_type=jnp.float32,
        )
        inner_sum = jnp.sum(
            grad_heads.astype(jnp.float32)
            * split_heads(attended_blk, head_count).astype(jnp.float32),
            axis=-1,
        ).T
        score_grad = (probabilities * (d_weights - inner_sum[..., None])).astype(jnp.bfloat16)
        d_query = (
            jnp.einsum(
                "hbk,khd->bhd",
                score_grad,
                split_heads(key_slots, head_count),
                preferred_element_type=jnp.float32,
            )
            * scaling
        )
        key_terms = (
            jnp.einsum(
                "hbk,bhd->khd",
                score_grad,
                split_heads(query_blk, head_count),
                preferred_element_type=jnp.float32,
            )
            * scaling
        )
        value_terms = jnp.einsum(
            "hbk,bhd->khd", weights, grad_heads, preferred_element_type=jnp.float32
        )
        return (
            d_query.astype(jnp.bfloat16).reshape(BLOCK, model_width),
            key_terms.reshape(-1, model_width),
            value_terms.reshape(-1, model_width),
        )

    query_grad_items, key_terms, value_terms = lax.map(
        backward_item, (query_items, flat_slots, count_items, attended_items, log_items, grad_items)
    )
    onehot = (
        neighbours.reshape(walk_dev, blocks * slot_count)[..., None]
        == jnp.arange(stored, dtype=jnp.int32)[None, None, :]
    ).astype(jnp.float32)

    def place(contribution):
        grouped = contribution.reshape(walk_dev, blocks * slot_count, BLOCK * model_width)
        placed = jnp.einsum("wsn,wsx->wnx", onehot, grouped, precision=lax.Precision.HIGHEST)
        return placed.reshape(walk_dev, stored, BLOCK, model_width).astype(jnp.bfloat16)

    key_round = place(key_terms)
    value_round = place(value_terms)
    key_wide = lax.optimization_barrier(key_round).astype(jnp.float32)
    value_wide = lax.optimization_barrier(value_round).astype(jnp.float32)
    key_sum, value_sum = (
        lax.psum_scatter(
            key_wide.astype(jnp.bfloat16), "elec", scatter_dimension=1, tiled=True
        ).astype(jnp.float32),
        lax.psum_scatter(
            value_wide.astype(jnp.bfloat16), "elec", scatter_dimension=1, tiled=True
        ).astype(jnp.float32),
    )
    key_grad_rows = key_sum.astype(jnp.bfloat16).reshape(-1, model_width)
    value_grad_rows = value_sum.astype(jnp.bfloat16).reshape(-1, model_width)
    query_grad_rows = query_grad_items.reshape(-1, model_width)
    grad_hidden = cot_rows.astype(jnp.float32) + jnp.dot(
        query_grad_rows, w_query.T, preferred_element_type=jnp.float32
    )
    grad_hidden = grad_hidden + jnp.dot(key_grad_rows, w_key.T, preferred_element_type=jnp.float32)
    grad_hidden = grad_hidden + jnp.dot(
        value_grad_rows, w_value.T, preferred_element_type=jnp.float32
    )
    grad_hidden = grad_hidden.astype(jnp.bfloat16).reshape(hidden.shape)
    grad_query = (
        jnp.dot(all_rows.T, query_grad_rows, preferred_element_type=jnp.float32) / walkers_all
    )
    grad_key = jnp.dot(all_rows.T, key_grad_rows, preferred_element_type=jnp.float32) / walkers_all
    grad_value = (
        jnp.dot(all_rows.T, value_grad_rows, preferred_element_type=jnp.float32) / walkers_all
    )
    grad_query, grad_key, grad_value, grad_out = lax.psum(
        (grad_query, grad_key, grad_value, grad_out), ("walk", "elec")
    )
    return (output.reshape(hidden.shape), grad_hidden, grad_query, grad_key, grad_value, grad_out)


F32 = jnp.float32
BF16 = jnp.bfloat16
PAIR = 2 * HD


def dot_nn(a, b):
    return lax.dot_general(a, b, (((1,), (0,)), ((), ())), preferred_element_type=F32)


def dot_nt(a, b):
    return lax.dot_general(a, b, (((1,), (1,)), ((), ())), preferred_element_type=F32)


def by_head(block):
    lane = lax.broadcasted_iota(jnp.int32, block.shape, 1)
    zero = jnp.zeros_like(block)
    return jnp.concatenate(
        [jnp.where(lane < HD, block, zero), jnp.where(lane < HD, zero, block)], axis=0
    )


def walker_kernel(
    nbr, cnt, hid, cot, wq_h, wk_h, wv_h, wo_h, out, grad, full,
    wq, wk, wv, wo, hs, cs, bs, bsend, q_s, k_s, v_s, da_s, kt_s, vt_s, dat_s,
    at_s, att_s, dqt_s, dq_s, w_s, ds_s, qb_s, db_s, kp_s, vp_s, dk_s, dv_s, ht_s, osend, gsend,
    g_s, a_s, r0, s1, b1, r1, zall, agxy,
    send_sem, recv_sem, local_sem, osem_s, osem_r, ar_send, ar_recv,
):
    e = lax.axis_index("elec")
    other = 1 - e
    blocks = hid.shape[1] // BLOCK
    slots = nbr.shape[2]
    n_blocks = 2 * blocks
    half = hid.shape[1]
    rows = 2 * half
    pairs = hid.shape[2] // PAIR

    walk = lax.axis_index("walk")
    planes = lax.axis_size("walk") // 4
    plane, spot = walk // 4, walk % 4
    sx, sy = spot % 2, spot // 2
    near = [((sy + r // 2) % 2) * 2 + (sx + r % 2) % 2 for r in range(1, 4)]
    layers = [(plane + r) % planes for r in range(1, planes)]
    spot_ids = [{"walk": plane * 4 + t, "elec": e} for t in near]
    layer_ids = [{"walk": t * 4 + spot, "elec": e} for t in layers]
    core_id = {"walk": walk, "elec": other}
    mesh_ids = pl.DeviceIdType.MESH

    barrier = pltpu.get_barrier_semaphore()
    for peer in [core_id] + spot_ids + layer_ids:
        pl.semaphore_signal(barrier, inc=1, device_id=peer, device_id_type=mesh_ids)

    local = [
        pltpu.make_async_copy(src, dst, local_sem.at[i])
        for i, (src, dst) in enumerate(
            (
                (hid.at[e], hs.at[e]), (wq_h, wq), (wk_h, wk), (wv_h, wv),
                (cot.at[e], cs.at[e]), (wo_h, wo),
            )
        )
    ]
    for copy in local:
        copy.start()

    lane = lax.broadcasted_iota(jnp.int32, (16, 128), 1)
    sub = lax.broadcasted_iota(jnp.int32, (16, 128), 0)
    for w in range(2):
        bias = jnp.full((16, 128), NEG_FILL, F32)
        for a in range(blocks):
            for j in range(slots):
                live = jnp.where(j < cnt[w, a], nbr[a, w, j], -1)
                bias = jnp.where((sub == a) & (lane == live), 0.0, bias)
        bsend[w] = bias.astype(BF16)

    pl.semaphore_wait(barrier, 3 + planes)
    sends = []
    for i, (src, dst) in enumerate(((hid, hs), (cot, cs), (bsend, bs))):
        copy = pltpu.make_async_remote_copy(
            src_ref=src.at[other], dst_ref=dst.at[e], send_sem=send_sem.at[i], recv_sem=recv_sem.at[i],
            device_id={"elec": other}, device_id_type=pl.DeviceIdType.MESH,
        )
        copy.start()
        sends.append(copy)

    bs[e] = bsend[e]
    for copy in local:
        copy.wait()

    def project(h):
        rows_h = hs[h]
        q_s[h] = (dot_nn(rows_h, wq[...]).astype(BF16).astype(F32) * HD ** (-0.5)).astype(BF16)
        k_s[h] = dot_nn(rows_h, wk[...]).astype(BF16)
        v_s[h] = dot_nn(rows_h, wv[...]).astype(BF16)
        da_s[h] = dot_nt(cs[h], wo[...]).astype(BF16)

    project(e)
    for copy in sends:
        copy.wait()
    project(other)

    k_all = k_s[...].reshape(rows, -1)
    v_all = v_s[...].reshape(rows, -1)
    kt = k_all.T
    vt = v_all.T
    dat = da_s[...].reshape(rows, -1).T
    which = (
        lax.broadcasted_iota(jnp.int32, (rows, 128), 0) // BLOCK
        == lax.broadcasted_iota(jnp.int32, (rows, 128), 1)
    )
    onehot = jnp.where(which, 1.0, 0.0).astype(BF16)
    for p in range(pairs):
        lanes = slice(p * PAIR, (p + 1) * PAIR)
        kp_s[p, :, :PAIR] = k_all[:, lanes]
        kp_s[p, :, PAIR:] = onehot
        vp_s[p] = v_all[:, lanes]
        kt_s[p] = kt[lanes]
        vt_s[p] = vt[lanes]
        for a in range(n_blocks):
            dat_s[p, a] = dat[lanes, a * BLOCK : (a + 1) * BLOCK]
            r = slice((a % blocks) * BLOCK, (a % blocks + 1) * BLOCK)
            qb_s[p, a // blocks, a % blocks] = by_head(q_s[a // blocks, r, lanes])
            db_s[p, a // blocks, a % blocks] = by_head(da_s[a // blocks, r, lanes])

    ht_s[...] = hs[...].reshape(rows, -1).T

    def group(p, g, hooks=None):
        for i in range(blocks):
            a = g * blocks + i
            q2 = qb_s[p, g, i]
            d2 = db_s[p, g, i]
            bias = jnp.broadcast_to(bs[g, i : i + 1, :], (2 * BLOCK, 128))
            scores = dot_nt(kp_s[p], jnp.concatenate([q2, bias], axis=1))
            top = jnp.max(scores, axis=0, keepdims=True)
            expo = jnp.exp(scores - top)
            prob = expo * (1.0 / jnp.sum(expo, axis=0, keepdims=True))
            weights = prob.astype(BF16)
            cols = slice(i * 2 * BLOCK, (i + 1) * 2 * BLOCK)
            w_s[:, cols] = weights
            mixed = dot_nn(vt_s[p], weights)
            att = jnp.concatenate([mixed[:HD, :BLOCK], mixed[HD:, BLOCK:]], axis=0).astype(BF16)
            prod = att.astype(F32) * dat_s[p, a].astype(F32)
            inner = jnp.concatenate(
                [
                    jnp.sum(prod[:HD], axis=0, keepdims=True),
                    jnp.sum(prod[HD:], axis=0, keepdims=True),
                ],
                axis=1,
            )
            at_s[p, a] = att
            att_s[p, g, i] = att.T
            d_scores = (prob * (dot_nt(vp_s[p], d2) - inner)).astype(BF16)
            ds_s[:, cols] = d_scores
            mixed = dot_nn(kt_s[p], d_scores)
            dqt = jnp.concatenate([mixed[:HD, :BLOCK], mixed[HD:, BLOCK:]], axis=0)
            dqt = (dqt * HD ** (-0.5)).astype(BF16)
            dqt_s[p, a] = dqt
            dq_s[p, g, i] = dqt.T
            if hooks and hooks[i]:
                hooks[i]()
        dk_s[g, p] = dot_nn(ds_s[...], qb_s[p, g].reshape(-1, PAIR)).astype(BF16)
        dv_s[g, p] = dot_nn(w_s[...], db_s[p, g].reshape(-1, PAIR)).astype(BF16)
    width = hid.shape[2]

    def summed(ref, p):
        return (ref[0, p].astype(F32) + ref[1, p].astype(F32)).astype(BF16)

    def weight_parts(p):
        lower = g_s.at[p, 0]
        upper = g_s.at[p, 1]
        lower[:width] = dot_nn(ht_s[...], dq_s[p].reshape(rows, PAIR))
        lower[width:] = dot_nn(ht_s[...], summed(dk_s, p))
        upper[:width] = dot_nn(ht_s[...], summed(dv_s, p))
        at = jnp.concatenate([at_s[p, a] for a in range(n_blocks)], axis=1)
        part = dot_nn(at, cs[...].reshape(rows, -1))
        for c in range(pairs):
            upper[pl.ds(width + c * PAIR, PAIR)] = part[:, c * PAIR : (c + 1) * PAIR]
        a_s[p] = g_s[p, other].astype(BF16)

    def transfers(stage, p):
        if stage == 0:
            todo = [(a_s.at[p], r0.at[p], core_id)]
        elif stage == 1:
            todo = [(b1.at[p, t], r1.at[p, r], spot_ids[r]) for r, t in enumerate(near)]
        elif stage == 2:
            todo = [(zall.at[p, plane], zall.at[p, plane], i) for i in layer_ids]
        elif stage == 3:
            todo = [(agxy.at[p, spot], agxy.at[p, spot], i) for i in spot_ids]
        else:
            todo = [(agxy.at[p], full.at[p, e], core_id)]
        return [
            pltpu.make_async_remote_copy(
                src_ref=src, dst_ref=dst, send_sem=ar_send.at[stage, p, r],
                recv_sem=ar_recv.at[stage, p, r], device_id=peer, device_id_type=mesh_ids,
            )
            for r, (src, dst, peer) in enumerate(todo)
        ]

    def begin(stage, p):
        for copy in transfers(stage, p):
            copy.start()

    def finish(stage, p):
        for copy in transfers(stage, p):
            copy.wait()
        if stage == 0:
            s1[p] = (g_s[p, e] + r0[p].astype(F32)).reshape(s1.shape[1:])
            b1[p] = s1[p].astype(BF16)
        elif stage == 1:
            total = s1[p, spot]
            for r in range(3):
                total = total + r1[p, r].astype(F32)
            zall[p, plane] = total.astype(BF16)
        elif stage == 2:
            total = zall[p, 0].astype(F32)
            for r in range(1, planes):
                total = total + zall[p, r].astype(F32)
            agxy[p, spot] = (total * (1.0 / (2 * lax.axis_size("walk")))).astype(BF16)
        elif stage == 3:
            full[p, e] = agxy[p]

    def advance(stage, p):
        finish(stage, p)
        begin(stage + 1, p)

    def first_pair(g, carry):
        group(0, g)
        return carry

    lax.fori_loop(0, 2, first_pair, 0)
    weight_parts(0)
    begin(0, 0)
    group(1, 0, [None, lambda: advance(0, 0), None])
    group(1, 1, [lambda: advance(1, 0), None, lambda: advance(2, 0)])
    weight_parts(1)
    begin(0, 1)

    def whole(ref):
        return jnp.concatenate([ref[p].reshape(rows, PAIR) for p in range(pairs)], axis=1)

    def give(i, src, dst):
        copy = pltpu.make_async_remote_copy(
            src_ref=src.at[other], dst_ref=dst.at[e], send_sem=osem_s.at[i], recv_sem=osem_r.at[i],
            device_id=core_id, device_id_type=mesh_ids,
        )
        copy.start()
        dst[e] = src[e]
        return copy

    result = (hs[...].reshape(rows, -1).astype(F32) + dot_nn(whole(att_s), wo[...])).astype(BF16)
    osend[...] = result.reshape(osend.shape)
    advance(0, 1)
    advance(3, 0)
    sends = [give(0, osend, out)]
    d_key = jnp.concatenate([summed(dk_s, p) for p in range(pairs)], axis=1)
    d_value = jnp.concatenate([summed(dv_s, p) for p in range(pairs)], axis=1)
    back = (
        cs[...].reshape(rows, -1).astype(F32)
        + dot_nt(whole(dq_s), wq[...])
        + dot_nt(d_key, wk[...])
        + dot_nt(d_value, wv[...])
    ).astype(BF16)
    gsend[...] = back.reshape(gsend.shape)
    advance(1, 1)
    sends.append(give(1, gsend, grad))
    finish(4, 0)
    advance(2, 1)
    advance(3, 1)
    for copy in sends:
        copy.wait()
    finish(4, 1)


def write_kernel(out, grad, full, out_h, grad_h, gq_h, gk_h, gv_h, go_h, gq, gk, gv, go, sem):
    copies = [pltpu.make_async_copy(out, out_h, sem.at[0]), pltpu.make_async_copy(grad, grad_h, sem.at[1])]
    for copy in copies:
        copy.start()
    width = gq.shape[0]
    pairs = full.shape[0]
    for t, (dst, dst_h) in enumerate(((gq, gq_h), (gk, gk_h), (gv, gv_h), (go, go_h))):
        for p in range(pairs):
            rows = full[p].reshape(4 * width, PAIR)[t * width : (t + 1) * width].astype(F32)
            if t < 3:
                dst[:, p * PAIR : (p + 1) * PAIR] = rows
            else:
                for c in range(pairs):
                    dst[p * PAIR : (p + 1) * PAIR, c * PAIR : (c + 1) * PAIR] = rows[c * PAIR : (c + 1) * PAIR]
        copies.append(pltpu.make_async_copy(dst, dst_h, sem.at[2 + t]))
        copies[-1].start()
    for copy in copies:
        copy.wait()


def pair_body(hidden, w_query, w_key, w_value, w_out, neighbours, counts, cotangent):
    half, width = hidden.shape[1:]
    blocks = half // BLOCK
    rows, pairs, n_blocks = 2 * half, width // PAIR, 2 * blocks
    vmem = pl.BlockSpec(memory_space=pltpu.VMEM)
    smem = pl.BlockSpec(memory_space=pltpu.SMEM)
    hbm = pl.BlockSpec(memory_space=pltpu.HBM)
    planes = lax.axis_size("walk") // 4
    peers = max(3, planes - 1)
    per = 4 * width // 2
    both = (2, half, width)
    by_pair = (pairs, 2, blocks, BLOCK, PAIR)
    by_pair2 = (pairs, 2, blocks, 2 * BLOCK, PAIR)

    def buf(*shape, dtype=BF16):
        return pltpu.VMEM(shape, dtype)

    out, grad, full = pl.pallas_call(
        walker_kernel,
        out_shape=(
            jax.ShapeDtypeStruct(hidden.shape, BF16),
            jax.ShapeDtypeStruct(hidden.shape, BF16),
            jax.ShapeDtypeStruct((pairs, 2, 4, per // 4, PAIR), BF16),
        ),
        in_specs=[smem, smem] + [hbm] * 6,
        out_specs=(vmem, vmem, vmem),
        scratch_shapes=[
            buf(width, width), buf(width, width), buf(width, width), buf(width, width),
            buf(*both), buf(*both), buf(2, 16, 128), buf(2, 16, 128),
            buf(*both), buf(*both), buf(*both), buf(*both),
            buf(pairs, PAIR, rows), buf(pairs, PAIR, rows), buf(pairs, n_blocks, PAIR, BLOCK),
            buf(pairs, n_blocks, PAIR, BLOCK), buf(*by_pair),
            buf(pairs, n_blocks, PAIR, BLOCK), buf(*by_pair),
            buf(rows, blocks * 2 * BLOCK), buf(rows, blocks * 2 * BLOCK),
            buf(*by_pair2), buf(*by_pair2),
            buf(pairs, rows, 2 * PAIR), buf(pairs, rows, PAIR),
            buf(2, pairs, rows, PAIR), buf(2, pairs, rows, PAIR),
            buf(width, rows), buf(*both), buf(*both),
            buf(pairs, 2, per, PAIR, dtype=F32), buf(pairs, per, PAIR), buf(pairs, per, PAIR),
            buf(pairs, 4, per // 4, PAIR, dtype=F32), buf(pairs, 4, per // 4, PAIR),
            buf(pairs, 3, per // 4, PAIR),
            buf(pairs, planes, per // 4, PAIR), buf(pairs, 4, per // 4, PAIR),
            pltpu.SemaphoreType.DMA((3,)), pltpu.SemaphoreType.DMA((3,)),
            pltpu.SemaphoreType.DMA((6,)),
            pltpu.SemaphoreType.DMA((2,)), pltpu.SemaphoreType.DMA((2,)),
            pltpu.SemaphoreType.DMA((5, pairs, peers)), pltpu.SemaphoreType.DMA((5, pairs, peers)),
        ],
        compiler_params=pltpu.CompilerParams(
            collective_id=0, has_side_effects=True, vmem_limit_bytes=62 * 1024 * 1024 + 768 * 1024
        ),
    )(neighbours.transpose(1, 0, 2), counts, hidden, cotangent, w_query, w_key, w_value, w_out)
    grads = jax.ShapeDtypeStruct((width, width), F32)
    return pl.pallas_call(
        write_kernel,
        out_shape=(
            jax.ShapeDtypeStruct(hidden.shape, BF16), jax.ShapeDtypeStruct(hidden.shape, BF16),
            grads, grads, grads, grads,
        ),
        in_specs=[vmem] * 3,
        out_specs=(hbm,) * 6,
        scratch_shapes=[buf(width, width, dtype=F32)] * 4 + [pltpu.SemaphoreType.DMA((6,))],
    )(out, grad, full)


def any_body(hidden, *rest):
    blocks = rest[4].shape[1]
    fits = hidden.shape[0] == 2 and hidden.shape[2] == 2 * PAIR and 2 * blocks <= 128 and blocks <= 16
    if fits and lax.axis_size("elec") == 2 and lax.axis_size("walk") in (8, 16):
        return pair_body(hidden, *rest)
    return body(hidden, *rest)


def solution(mesh):
    placed = (
        P("walk", "elec", None),
        P(),
        P(),
        P(),
        P(),
        P("walk", "elec", None),
        P("walk", "elec"),
        P("walk", "elec", None),
    )
    return jax.shard_map(
        any_body,
        mesh=mesh,
        in_specs=placed,
        out_specs=(P("walk", "elec", None), P("walk", "elec", None), P(), P(), P(), P()),
        check_vma=False,
    )
```
